32 devices in a mesh: seq: 8 (over z, x), doc: 4 (over y, core).
Axes of the slice: x: 2, y: 2, z: 4, core: 2. Of those that a mesh axis runs over, the one named last changes fastest.
Arguments:
- values: bfloat16 [4, 2048, 4096], P('doc', 'seq'), may hold values from -6 to 6
- b_in: bfloat16 [4, 2048, 128], P('doc', 'seq'), may hold values from -0.032958984 to 0.032958984
- c_in: bfloat16 [4, 2048, 128], P('doc', 'seq'), may hold values from -6 to 6
- log_decay: float32 [4, 64, 2048], P('doc', None, 'seq'), may hold values from -1 to 0, as said below
- skip: float32 [64], replicated, may hold values from 0.5 to 1.5
- owner: int32 [4, 16], P(None, 'seq'), may hold values from -1 to 3, as said below
Outputs:
- owned: bfloat16 [4, 64, 128, 4096], P('doc', 'seq')
The draws below stay inside these ranges and needn't reach their ends.
Inputs may be any that keep to these rules, and one draw needn't show every extreme that they name: `log_decay`: all entries are at most 0. In each head the per-token rates vary from token to token and from shard to shard. Within each shard of 2 blocks of a document, both blocks name the same owner (so no block is marked -1); in general -1 marks a block that is not kept.
All inputs are finite; a program needn't handle non-finite values.
Results may differ from the reference program's by a relative error of at most 0.0063.
Values may be sent and summed in bfloat16 or wider, within the bound.
A program may use at most 192 MiB of HBM per device.

```python
import functools
import jax
import jax.numpy as jnp
from jax import lax

HEADS = 64
HDIM = 64
NSTATE = 128
Q = 128
CAP = 2
L_DEV = 256
BLK_DEV = 2
TEXT_NUMBER = 4
WORDS_IN_TEXT = 2048
BLOCKS = 16
N_SEQ = 8


def draw_log_decay(key, part):
    random_seed_chain = jax.random.split(jax.random.fold_in(key, 7), 5)
    shard_count = WORDS_IN_TEXT // L_DEV
    slow_share = 0.5
    lagging_channels = jax.random.uniform(random_seed_chain[0], (TEXT_NUMBER, HEADS, 1)) < slow_share
    factor_each_slice = jnp.exp(jax.random.uniform(random_seed_chain[1], (TEXT_NUMBER, HEADS, shard_count), minval=-0.7, maxval=0.7))
    factor_each_slice = jnp.repeat(factor_each_slice, L_DEV, axis=2)
    noise_amplitude = jnp.exp(jax.random.uniform(random_seed_chain[2], (TEXT_NUMBER, HEADS, WORDS_IN_TEXT), minval=-0.7, maxval=0.7))
    floor_speed = jnp.where(lagging_channels, 0.3 / WORDS_IN_TEXT, 0.03)
    spike_place = jax.random.randint(random_seed_chain[3], (TEXT_NUMBER, 3), 0, WORDS_IN_TEXT)
    spike_magnitude = jax.random.uniform(random_seed_chain[4], (TEXT_NUMBER, 3), minval=0.22, maxval=0.45)
    word_offsets = jnp.arange(WORDS_IN_TEXT)
    spike_happenings = jnp.sum(jnp.where(word_offsets[None, :, None] == spike_place[:, None, :], spike_magnitude[:, None, :], 0.0), axis=2)
    fading_factors = floor_speed * factor_each_slice * noise_amplitude + jnp.where(lagging_channels, spike_happenings[:, None, :], 0.0)
    return (-fading_factors).astype(jnp.float32)


def draw_owner(key, part):
    random_seed_chain = jax.random.split(jax.random.fold_in(key, 11), 3)
    shard_count = BLOCKS // BLK_DEV
    hot_owner = jax.random.randint(random_seed_chain[0], (TEXT_NUMBER, shard_count, 1), 0, TEXT_NUMBER)
    extra_counts = jax.random.randint(random_seed_chain[1], (TEXT_NUMBER, shard_count, TEXT_NUMBER), 0, CAP + 1)
    rank_ids = jnp.arange(TEXT_NUMBER)
    counts = jnp.where(rank_ids[None, None, :] == 0, CAP, extra_counts)
    slot_ids = jnp.arange(BLK_DEV)
    rank_of = slot_ids // CAP
    within = slot_ids % CAP
    wanted = jnp.take(counts, jnp.minimum(rank_of, TEXT_NUMBER - 1), axis=2)
    usable = (rank_of[None, None, :] < TEXT_NUMBER) & (within[None, None, :] < wanted)
    labels = jnp.where(usable, (hot_owner + rank_of[None, None, :]) % TEXT_NUMBER, -1)
    labels = labels.reshape(TEXT_NUMBER * shard_count, BLK_DEV)
    perm_keys = jax.random.split(random_seed_chain[2], TEXT_NUMBER * shard_count)
    orders = jax.vmap(lambda one_key: jax.random.permutation(one_key, BLK_DEV))(perm_keys)
    shuffled = jnp.take_along_axis(labels, orders, axis=1)
    return shuffled.reshape(TEXT_NUMBER, BLOCKS).astype(jnp.int32)


def levels(key, dims, cuts, smallest, largest):
    level = 1.0
    for position, shards_of in cuts:
        steps = jax.random.uniform(jax.random.fold_in(jax.random.fold_in(key, 6), position), (shards_of,), jnp.float32, smallest / len(cuts), largest / len(cuts))
        level = level * jnp.repeat(jnp.exp(steps), dims[position] // shards_of).reshape((-1,) + (1,) * (len(dims) - 1 - position))
    return level


def scatter_about(key, dims, spread, limit, cuts=(), kind=jnp.bfloat16):
    entries = spread * jax.random.normal(key, dims, jnp.float32)
    if cuts:
        entries = entries * levels(key, dims, cuts, -0.22, 0.18)
    return jnp.clip(entries, -limit, limit).astype(kind)


def setup_inputs(seed: int = 0) -> dict:
    streams_of = jax.random.split(jax.random.key(seed), 7)
    return {
        "values": scatter_about(streams_of[0], (TEXT_NUMBER, WORDS_IN_TEXT, HEADS * HDIM), 1.0, 6.0, ((0, 4), (1, 8))),
        "b_in": scatter_about(streams_of[1], (TEXT_NUMBER, WORDS_IN_TEXT, NSTATE), (1.0 / (NSTATE * L_DEV) ** 0.5), 0.032958984, ((0, 4), (1, 8))),
        "c_in": scatter_about(streams_of[2], (TEXT_NUMBER, WORDS_IN_TEXT, NSTATE), 1.0, 6.0, ((0, 4), (1, 8))),
        "log_decay": draw_log_decay(jax.random.fold_in(streams_of[6], 71), 0),
        "skip": jnp.clip(jax.random.uniform(streams_of[4], (HEADS,), jnp.float32, 0.5, 1.5), 0.5, 1.5),
        "owner": draw_owner(jax.random.fold_in(streams_of[6], 71), 0),
    }


def block_pass(carried, inputs, skip):
    value_block, b_block, c_block, decay_block = inputs
    head_count = decay_block.shape[0]
    row_width = value_block.shape[1]
    head_dim = row_width // head_count
    cum_decay = jnp.cumsum(decay_block, axis=1)
    scores = jnp.dot(c_block, b_block.T, preferred_element_type=jnp.float32)
    row_ids = jnp.arange(Q)
    lower_mask = row_ids[:, None] >= row_ids[None, :]
    decay_gap = cum_decay[:, :, None] - cum_decay[:, None, :]
    weights = jnp.where(lower_mask, scores[None] * jnp.exp(jnp.where(lower_mask, decay_gap, 0.0)), 0.0).astype(jnp.bfloat16)
    weights = lax.optimization_barrier(weights)
    value_heads = value_block.reshape(Q, head_count, head_dim).astype(jnp.float32)
    diagonal = jnp.einsum("hts,shp->thp", weights.astype(jnp.float32), value_heads)
    c_weighted = (c_block.astype(jnp.float32)[None] * jnp.exp(cum_decay)[:, :, None]).astype(jnp.bfloat16)
    enter_state = carried.astype(jnp.bfloat16)
    c_weighted, enter_state = lax.optimization_barrier((c_weighted, enter_state))
    carried_term = jnp.einsum("htn,hnp->thp", c_weighted.astype(jnp.float32), enter_state.astype(jnp.float32))
    out_block = (diagonal + carried_term + skip[None, :, None] * value_heads).reshape(Q, row_width).astype(jnp.bfloat16)
    b_weighted = (b_block.astype(jnp.float32)[None] * jnp.exp(cum_decay[:, -1:] - cum_decay)[:, :, None]).astype(jnp.bfloat16)
    b_weighted = lax.optimization_barrier(b_weighted)
    local_state = jnp.einsum("hsn,shp->hnp", b_weighted.astype(jnp.float32), value_heads)
    new_state = jnp.exp(cum_decay[:, -1])[:, None, None] * carried + local_state
    return new_state, out_block


def reference(values, b_in, c_in, log_decay, skip, owner):
    doc_count = values.shape[0]
    seq_len = values.shape[1]
    row_width = values.shape[2]
    head_count = log_decay.shape[1]
    head_dim = row_width // head_count
    state_dim = b_in.shape[2]
    block_count = seq_len // Q
    shard_blocks = block_count // N_SEQ
    step_fn = functools.partial(block_pass, skip=skip)
    picked_docs = []
    for doc_index in range(doc_count):
        value_rows = values[doc_index].reshape(block_count, Q, row_width)
        b_rows = b_in[doc_index].reshape(block_count, Q, state_dim)
        c_rows = c_in[doc_index].reshape(block_count, Q, state_dim)
        decay_rows = log_decay[doc_index].reshape(head_count, block_count, Q).transpose(1, 0, 2)
        start_state = jnp.zeros((head_count, state_dim, head_dim), jnp.float32)
        final_state, out_blocks = lax.scan(step_fn, start_state, (value_rows, b_rows, c_rows, decay_rows))
        shard_rows = out_blocks.reshape(N_SEQ, shard_blocks, Q, row_width)
        owner_rows = owner[doc_index].reshape(N_SEQ, shard_blocks)
        owner_ids = jnp.arange(doc_count, dtype=jnp.int32)
        matches = (owner_rows[:, None, :] == owner_ids[None, :, None]).astype(jnp.int32)
        ranking = jnp.cumsum(matches, axis=2) - 1
        slot_ids = jnp.arange(CAP, dtype=jnp.int32)
        chosen = (matches[:, :, None, :] > 0) & (ranking[:, :, None, :] == slot_ids[None, None, :, None])
        block_ids = jnp.arange(shard_blocks, dtype=jnp.int32)
        source_index = jnp.sum(jnp.where(chosen, block_ids, 0), axis=3).astype(jnp.int32)
        present = jnp.any(chosen, axis=3)
        shard_ids = jnp.arange(N_SEQ, dtype=jnp.int32)
        picked = shard_rows[shard_ids[:, None, None], source_index]
        picked = jnp.where(present[:, :, :, None, None], picked, jnp.zeros((), picked.dtype))
        picked_docs.append(picked)
    stacked = jnp.stack(picked_docs)
    return stacked.transpose(2, 1, 0, 3, 4, 5).reshape(doc_count, N_SEQ * doc_count * CAP, Q, row_width)
```

```python
import functools

import jax
import jax.numpy as jnp
from jax import lax
from jax.experimental import pallas as pl
from jax.experimental.pallas import tpu as pltpu
from jax.sharding import PartitionSpec as P

Q = 128
CAP = 2
MESH = pl.DeviceIdType.MESH
F32 = jnp.float32
BF16 = jnp.bfloat16


def layer_kernel(
    n_seq, n_doc, heads, width, chunks,
    v_hbm, b_ref, c_ref, ld_ref, skip_ref, gathered,
    v_buf, lhs_buf, sb_buf, a_buf, d_buf, row_buf, l_buf, x_out, x_in, z_out, z_in, o_buf,
    v_sem, own_sem, xs, xr, zs, zr, ys, yr, cs, cr, fs, fr,
):
    seq_len, row_width = v_buf.shape
    blocks = seq_len // Q
    state_dim = b_ref.shape[1]
    head_dim = row_width // heads
    sides = n_doc // 2
    rungs = n_seq // 2
    seq = lax.axis_index("seq")
    doc = lax.axis_index("doc")
    rung, second = seq // 2, seq % 2
    side, core = doc // 2, doc % 2
    across = (seq + 1 - 2 * second, doc)
    above = (seq + 2, doc)
    below = (seq - 2, doc)
    twin = (seq, doc + 1 - 2 * core)
    far = [(seq, ((side + j) % sides) * 2 + core) for j in range(1, sides)]

    load = pltpu.make_async_copy(v_hbm, v_buf, v_sem)
    load.start()

    barrier = pltpu.get_barrier_semaphore()
    for other in [across, twin] + far:
        pl.semaphore_signal(barrier, inc=1, device_id=other, device_id_type=MESH)

    @pl.when(rung > 0)
    def _():
        pl.semaphore_signal(barrier, inc=1, device_id=below, device_id_type=MESH)

    @pl.when(rung < rungs - 1)
    def _():
        pl.semaphore_signal(barrier, inc=1, device_id=above, device_id_type=MESH)

    rows_i = lax.broadcasted_iota(jnp.int32, (Q, Q), 0)
    cols_i = lax.broadcasted_iota(jnp.int32, (Q, Q), 1)
    lower = rows_i >= cols_i
    ones_lower = jnp.where(lower, 1.0, 0.0).astype(F32)
    lane = lax.broadcasted_iota(jnp.int32, (1, 2 * heads), 1)
    twice = (
        lax.broadcasted_iota(jnp.int32, (heads, 2 * heads), 1) % heads
        == lax.broadcasted_iota(jnp.int32, (heads, 2 * heads), 0)
    )
    skip_row = jnp.dot(
        jnp.broadcast_to(skip_ref[...], (8, heads)), jnp.where(twice, 1.0, 0.0).astype(F32),
        precision=lax.Precision.HIGHEST, preferred_element_type=F32,
    )[0:1]

    def split(x):
        high = x.astype(BF16).astype(F32)
        return jnp.where(lane < heads, high, x - high).astype(BF16)

    small = [skip_row]
    halves, totals, befores = [], [], []
    running = jnp.zeros((1, 2 * heads), F32)
    for k in range(blocks):
        span = slice(k * Q, (k + 1) * Q)
        decay = ld_ref[:, span]
        decay = jnp.concatenate([decay, decay], axis=0)
        cum = lax.dot_general(
            ones_lower, decay, (((1,), (1,)), ((), ())),
            precision=lax.Precision.HIGHEST, preferred_element_type=F32,
        )
        total = cum[Q - 1:Q]
        half = 0.5 * total
        lhs_buf[2 * k * Q:(2 * k + 1) * Q, :] = split(jnp.exp(cum - half))
        lhs_buf[(2 * k + 1) * Q:(2 * k + 2) * Q, :] = split(jnp.exp(half - cum))
        running = running + total
        halves.append(jnp.exp(half))
        totals.append(jnp.exp(total))
        befores.append(jnp.exp(running))
        b_block = b_ref[span, :]
        scores = lax.dot_general(
            c_ref[span, :], b_block, (((1,), (1,)), ((), ())), preferred_element_type=F32
        )
        sb_buf[k, 0:Q, :] = jnp.where(lower, scores, 0.0).astype(BF16)
        sb_buf[k, Q:Q + state_dim, :] = b_block.astype(F32).T.astype(BF16)
    small = [skip_row] + halves + totals + befores
    row_count = row_buf.shape[1]
    row_id = lax.broadcasted_iota(jnp.int32, (row_count, 2 * heads), 0)
    stacked = jnp.zeros((row_count, 2 * heads), F32)
    for i, row in enumerate(small):
        stacked = jnp.where(row_id == i, row, stacked)
    base = 2 * blocks * Q
    lhs_buf[base:base + row_count, :] = split(stacked)

    @pl.when(rung == 0)
    def _():
        z_in[...] = jnp.zeros_like(z_in)

    peers = 2 + len(far) + jnp.where(rung > 0, 1, 0) + jnp.where(rung < rungs - 1, 1, 0)
    pl.semaphore_wait(barrier, peers)
    load.wait()

    def x_copy(g):
        return pltpu.make_async_remote_copy(
            x_out.at[g], x_in.at[g], xs.at[g], xr.at[g], device_id=across, device_id_type=MESH)

    def z_copy(g):
        return pltpu.make_async_remote_copy(
            z_out.at[g], z_in.at[g], zs.at[g], zr.at[g], device_id=above, device_id_type=MESH)

    def far_copy(j, g):
        return pltpu.make_async_remote_copy(
            o_buf.at[g], gathered.at[doc, g], ys.at[j, g], yr.at[j, g],
            device_id=far[j], device_id_type=MESH)

    def twin_copy(g):
        return pltpu.make_async_remote_copy(
            o_buf.at[g], gathered.at[doc, g], cs.at[g], cr.at[g],
            device_id=twin, device_id_type=MESH)

    def own_copy(g):
        return pltpu.make_async_copy(o_buf.at[g], gathered.at[doc, g], own_sem.at[g])

    def forward_copy(j, g):
        source = ((side + sides - 1 - j) % sides) * 2 + core
        return pltpu.make_async_remote_copy(
            gathered.at[source, g], gathered.at[source, g], fs.at[j, g], fr.at[j, g],
            device_id=twin, device_id_type=MESH)

    def local_part(g, carry):
        lanes = pl.ds(pl.multiple_of(g * width, width), width)
        head_of = lax.broadcasted_iota(jnp.int32, (2 * heads, width), 1) // head_dim
        head_at = lax.broadcasted_iota(jnp.int32, (2 * heads, width), 0) % heads
        spread = jnp.where(head_at == head_of + g * (width // head_dim), 1.0, 0.0).astype(BF16)
        rows = jnp.dot(lhs_buf[base:base + row_count, :], spread, preferred_element_type=F32)
        row_buf[g] = rows
        state = jnp.zeros((state_dim, width), F32)
        for k in range(blocks):
            a_buf[g, k * Q:(k + 1) * Q, :] = jnp.dot(
                lhs_buf[2 * k * Q:(2 * k + 1) * Q, :], spread, preferred_element_type=F32)
            grow = jnp.dot(
                lhs_buf[(2 * k + 1) * Q:(2 * k + 2) * Q, :], spread, preferred_element_type=F32)
            scaled = (v_buf[k * Q:(k + 1) * Q, lanes].astype(F32) * grow).astype(BF16)
            both = jnp.dot(sb_buf[k], scaled, preferred_element_type=F32)
            d_buf[g, k * Q:(k + 1) * Q, :] = both[0:Q]
            state = rows[1 + blocks + k:2 + blocks + k] * state + rows[1 + k:2 + k] * both[Q:]
            l_buf[k, g] = state
        x_out[g, 0:state_dim, :] = state.astype(BF16)
        decay = rows[3 * blocks:3 * blocks + 1]
        high = decay.astype(BF16).astype(F32)
        tail = lax.broadcasted_iota(jnp.int32, (16, width), 0)
        x_out[g, state_dim:state_dim + 16, :] = jnp.where(
            tail == 0, high, jnp.where(tail == 1, decay - high, 0.0)).astype(BF16)
        x_copy(g).start()
        return carry

    lax.fori_loop(0, chunks, local_part, 0)

    def carried_part(g, carry):
        lanes = pl.ds(pl.multiple_of(g * width, width), width)
        rows = row_buf[g]
        x_copy(g).wait_recv()
        other = x_in[g, 0:state_dim, :].astype(F32)
        other_tail = x_in[g, state_dim:state_dim + 16, :].astype(F32)
        other_decay = other_tail[0:1] + other_tail[1:2]
        mine = l_buf[blocks - 1, g]
        mine_decay = rows[3 * blocks:3 * blocks + 1]
        is_second = second == 1
        first_state = jnp.where(is_second, other, mine)
        last_state = jnp.where(is_second, mine, other)
        first_decay = jnp.where(is_second, other_decay, mine_decay)
        last_decay = jnp.where(is_second, mine_decay, other_decay)

        @pl.when(rung > 0)
        def _():
            z_copy(g).wait_recv()

        enter = z_in[g].astype(F32)
        middle = first_decay * enter + first_state

        @pl.when(rung < rungs - 1)
        def _():
            z_out[g] = (last_decay * middle + last_state).astype(BF16)
            z_copy(g).start()

        enter = jnp.where(is_second, middle, enter)
        skip_lanes = rows[0:1]
        for k in range(blocks):
            span = slice(k * Q, (k + 1) * Q)
            at_block = enter
            if k > 0:
                at_block = rows[2 * blocks + k:2 * blocks + k + 1] * enter + l_buf[k - 1, g]
            scaled = (rows[1 + k:2 + k] * at_block).astype(BF16)
            inner = d_buf[g, span, :] + jnp.dot(
                c_ref[span, :], scaled, preferred_element_type=F32)
            o_buf[g, span, :] = (
                a_buf[g, span, :] * inner + skip_lanes * v_buf[span, lanes].astype(F32)
            ).astype(BF16)
        for j in range(len(far)):
            far_copy(j, g).start()
        twin_copy(g).start()
        own_copy(g).start()
        return carry

    lax.fori_loop(0, chunks, carried_part, 0)

    def forward(g, carry):
        for j in range(len(far)):
            far_copy(j, g).wait_recv()
            forward_copy(j, g).start()
        return carry

    lax.fori_loop(0, chunks, forward, 0)

    def finish(g, carry):
        x_copy(g).wait_send()

        @pl.when(rung < rungs - 1)
        def _():
            z_copy(g).wait_send()

        for j in range(len(far)):
            far_copy(j, g).wait_send()
            forward_copy(j, g).wait()
        twin_copy(g).wait()
        own_copy(g).wait()
        return carry

    lax.fori_loop(0, chunks, finish, 0)


def slot_source(index, owner, me, blocks):
    doc, rank = index // CAP, index % CAP
    seen = jnp.int32(0)
    block = jnp.int32(0)
    present = jnp.bool_(False)
    for j in range(blocks):
        match = owner[doc * blocks + j] == me
        hit = match & (seen == rank)
        block = jnp.where(hit, j, block)
        present = present | hit
        seen = seen + match.astype(jnp.int32)
    return present, doc, block


def pick_kernel(blocks, owner, me, taken, out):
    present, _, _ = slot_source(pl.program_id(0), owner, me[0], blocks)
    chunks, width = taken.shape[1], taken.shape[3]

    @pl.when(present)
    def _():
        for g in range(chunks):
            out[0, 0, :, g * width:(g + 1) * width] = taken[0, g]

    @pl.when(jnp.logical_not(present))
    def _():
        out[...] = jnp.zeros_like(out)


def local(n_seq, n_doc, values, b_in, c_in, log_decay, skip, owner):
    seq_len, row_width = values.shape[1], values.shape[2]
    heads = log_decay.shape[1]
    state_dim = b_in.shape[2]
    blocks = seq_len // Q
    width = min(256, row_width)
    chunks = row_width // width
    far = n_doc // 2 - 1
    row_count = -(-(1 + 3 * blocks) // 16) * 16
    vmem = pl.BlockSpec(memory_space=pltpu.VMEM)
    anywhere = pl.BlockSpec(memory_space=pl.ANY)
    dma = pltpu.SemaphoreType.DMA
    gathered = pl.pallas_call(
        functools.partial(layer_kernel, n_seq, n_doc, heads, width, chunks),
        out_shape=jax.ShapeDtypeStruct((n_doc, chunks, seq_len, width), BF16),
        in_specs=[anywhere, vmem, vmem, vmem, vmem],
        out_specs=anywhere,
        scratch_shapes=[
            pltpu.VMEM((seq_len, row_width), BF16),
            pltpu.VMEM((2 * seq_len + row_count, 2 * heads), BF16),
            pltpu.VMEM((blocks, Q + state_dim, Q), BF16),
            pltpu.VMEM((chunks, seq_len, width), F32),
            pltpu.VMEM((chunks, seq_len, width), F32),
            pltpu.VMEM((chunks, row_count, width), F32),
            pltpu.VMEM((blocks, chunks, state_dim, width), F32),
            pltpu.VMEM((chunks, state_dim + 16, width), BF16),
            pltpu.VMEM((chunks, state_dim + 16, width), BF16),
            pltpu.VMEM((chunks, state_dim, width), BF16),
            pltpu.VMEM((chunks, state_dim, width), BF16),
            pltpu.VMEM((chunks, seq_len, width), BF16),
            dma(()),
            dma((chunks,)),
            dma((chunks,)),
            dma((chunks,)),
            dma((chunks,)),
            dma((chunks,)),
            dma((far, chunks)),
            dma((far, chunks)),
            dma((chunks,)),
            dma((chunks,)),
            dma((far, chunks)),
            dma((far, chunks)),
        ],
        compiler_params=pltpu.CompilerParams(
            collective_id=0, has_side_effects=True, vmem_limit_bytes=44 * 2**20
        ),
        name="layer",
    )(values[0], b_in[0], c_in[0], log_decay[0], skip.reshape(1, heads))

    slots = n_doc * CAP
    me = lax.axis_index("doc").astype(jnp.int32).reshape(1)

    def taken_at(i, owner, me):
        doc_at, block_at = jnp.int32(0), jnp.int32(0)
        for j in range(slots):
            present, doc, block = slot_source(j, owner, me[0], blocks)
            use = present & (j <= i)
            doc_at = jnp.where(use, doc, doc_at)
            block_at = jnp.where(use, block, block_at)
        return doc_at, 0, block_at, 0

    return pl.pallas_call(
        functools.partial(pick_kernel, blocks),
        out_shape=jax.ShapeDtypeStruct((1, slots, Q, row_width), BF16),
        grid_spec=pltpu.PrefetchScalarGridSpec(
            num_scalar_prefetch=2,
            grid=(slots,),
            in_specs=[pl.BlockSpec((1, chunks, Q, width), taken_at)],
            out_specs=pl.BlockSpec((1, 1, Q, row_width), lambda i, owner, me: (0, i, 0, 0)),
        ),
        compiler_params=pltpu.CompilerParams(vmem_limit_bytes=16 * 2**20),
        name="pick",
    )(owner.reshape(-1), me, gathered)


def solution(mesh):
    in_specs = (
        P("doc", "seq", None),
        P("doc", "seq", None),
        P("doc", "seq", None),
        P("doc", None, "seq"),
        P(),
        P(None, "seq"),
    )
    out_specs = P("doc", "seq", None, None)
    body = functools.partial(local, mesh.shape["seq"], mesh.shape["doc"])
    return jax.shard_map(body, mesh=mesh, in_specs=in_specs, out_specs=out_specs, check_vma=False)
```

```python
import functools

import jax
import jax.numpy as jnp
from jax import lax
from jax.experimental import pallas as pl
from jax.experimental.pallas import tpu as pltpu
from jax.sharding import PartitionSpec as P

Q = 128
CAP = 2
MESH = pl.DeviceIdType.MESH
F32 = jnp.float32
BF16 = jnp.bfloat16


def layer_kernel(
    n_seq, n_doc, heads, width, chunks,
    v_hbm, b_hbm, c_hbm, ld_hbm, skip_hbm, gathered,
    v_buf, b_ref, c_ref, ld_ref, skip_ref, lhs_buf, sb_buf, a_buf, d_buf, row_buf, l_buf, x_out, x_in, z_out, z_in, o_buf,
    in_sem, own_sem, xs, xr, zs, zr, ys, yr, cs, cr, fs, fr,
):
    seq_len, row_width = v_buf.shape
    blocks = seq_len // Q
    state_dim = b_ref.shape[1]
    head_dim = row_width // heads
    sides = n_doc // 2
    rungs = n_seq // 2
    seq = lax.axis_index("seq")
    doc = lax.axis_index("doc")
    rung, second = seq // 2, seq % 2
    side, core = doc // 2, doc % 2
    across = (seq + 1 - 2 * second, doc)
    above = (seq + 2, doc)
    below = (seq - 2, doc)
    twin = (seq, doc + 1 - 2 * core)
    far = [(seq, ((side + j) % sides) * 2 + core) for j in range(1, sides)]

    pairs = [(ld_hbm, ld_ref), (skip_hbm, skip_ref), (b_hbm, b_ref), (c_hbm, c_ref), (v_hbm, v_buf)]
    loads = [pltpu.make_async_copy(a, b, in_sem.at[i]) for i, (a, b) in enumerate(pairs)]
    for load in loads:
        load.start()

    barrier = pltpu.get_barrier_semaphore()
    for other in [across, twin] + far:
        pl.semaphore_signal(barrier, inc=1, device_id=other, device_id_type=MESH)

    @pl.when(rung > 0)
    def _():
        pl.semaphore_signal(barrier, inc=1, device_id=below, device_id_type=MESH)

    @pl.when(rung < rungs - 1)
    def _():
        pl.semaphore_signal(barrier, inc=1, device_id=above, device_id_type=MESH)

    for load in loads[:-1]:
        load.wait()

    rows_i = lax.broadcasted_iota(jnp.int32, (Q, Q), 0)
    cols_i = lax.broadcasted_iota(jnp.int32, (Q, Q), 1)
    lower = rows_i >= cols_i
    ones_lower = jnp.where(lower, 1.0, 0.0).astype(F32)
    lane = lax.broadcasted_iota(jnp.int32, (1, 2 * heads), 1)
    twice = (
        lax.broadcasted_iota(jnp.int32, (heads, 2 * heads), 1) % heads
        == lax.broadcasted_iota(jnp.int32, (heads, 2 * heads), 0)
    )
    skip_row = jnp.dot(
        jnp.broadcast_to(skip_ref[...], (8, heads)), jnp.where(twice, 1.0, 0.0).astype(F32),
        precision=lax.Precision.HIGHEST, preferred_element_type=F32,
    )[0:1]

    def split(x):
        high = x.astype(BF16).astype(F32)
        return jnp.where(lane < heads, high, x - high).astype(BF16)

    small = [skip_row]
    halves, totals, befores = [], [], []
    running = jnp.zeros((1, 2 * heads), F32)
    for k in range(blocks):
        span = slice(k * Q, (k + 1) * Q)
        decay = ld_ref[:, span]
        decay = jnp.concatenate([decay, decay], axis=0)
        cum = lax.dot_general(
            ones_lower, decay, (((1,), (1,)), ((), ())),
            precision=lax.Precision.HIGHEST, preferred_element_type=F32,
        )
        total = cum[Q - 1:Q]
        half = 0.5 * total
        lhs_buf[2 * k * Q:(2 * k + 1) * Q, :] = split(jnp.exp(cum - half))
        lhs_buf[(2 * k + 1) * Q:(2 * k + 2) * Q, :] = split(jnp.exp(half - cum))
        running = running + total
        halves.append(jnp.exp(half))
        totals.append(jnp.exp(total))
        befores.append(jnp.exp(running))
        b_block = b_ref[span, :]
        scores = lax.dot_general(
            c_ref[span, :], b_block, (((1,), (1,)), ((), ())), preferred_element_type=F32
        )
        sb_buf[k, 0:Q, :] = jnp.where(lower, scores, 0.0).astype(BF16)
        sb_buf[k, Q:Q + state_dim, :] = b_block.astype(F32).T.astype(BF16)
    small = [skip_row] + halves + totals + befores
    row_count = row_buf.shape[1]
    row_id = lax.broadcasted_iota(jnp.int32, (row_count, 2 * heads), 0)
    stacked = jnp.zeros((row_count, 2 * heads), F32)
    for i, row in enumerate(small):
        stacked = jnp.where(row_id == i, row, stacked)
    base = 2 * blocks * Q
    lhs_buf[base:base + row_count, :] = split(stacked)

    @pl.when(rung == 0)
    def _():
        z_in[...] = jnp.zeros_like(z_in)

    peers = 2 + len(far) + jnp.where(rung > 0, 1, 0) + jnp.where(rung < rungs - 1, 1, 0)
    pl.semaphore_wait(barrier, peers)
    loads[-1].wait()

    def x_copy(g):
        return pltpu.make_async_remote_copy(
            x_out.at[g], x_in.at[g], xs.at[g], xr.at[g], device_id=across, device_id_type=MESH)

    def z_copy(g):
        return pltpu.make_async_remote_copy(
            z_out.at[g], z_in.at[g], zs.at[g], zr.at[g], device_id=above, device_id_type=MESH)

    def far_copy(j, g):
        return pltpu.make_async_remote_copy(
            o_buf.at[g], gathered.at[doc, g], ys.at[j, g], yr.at[j, g],
            device_id=far[j], device_id_type=MESH)

    def twin_copy(g):
        return pltpu.make_async_remote_copy(
            o_buf.at[g], gathered.at[doc, g], cs.at[g], cr.at[g],
            device_id=twin, device_id_type=MESH)

    def own_copy(g):
        return pltpu.make_async_copy(o_buf.at[g], gathered.at[doc, g], own_sem.at[g])

    def forward_copy(j, g):
        source = ((side + sides - 1 - j) % sides) * 2 + core
        return pltpu.make_async_remote_copy(
            gathered.at[source, g], gathered.at[source, g], fs.at[j, g], fr.at[j, g],
            device_id=twin, device_id_type=MESH)

    def local_part(g, carry):
        lanes = pl.ds(pl.multiple_of(g * width, width), width)
        head_of = lax.broadcasted_iota(jnp.int32, (2 * heads, width), 1) // head_dim
        head_at = lax.broadcasted_iota(jnp.int32, (2 * heads, width), 0) % heads
        spread = jnp.where(head_at == head_of + g * (width // head_dim), 1.0, 0.0).astype(BF16)
        rows = jnp.dot(lhs_buf[base:base + row_count, :], spread, preferred_element_type=F32)
        row_buf[g] = rows
        state = jnp.zeros((state_dim, width), F32)
        for k in range(blocks):
            a_buf[g, k * Q:(k + 1) * Q, :] = jnp.dot(
                lhs_buf[2 * k * Q:(2 * k + 1) * Q, :], spread, preferred_element_type=F32)
            grow = jnp.dot(
                lhs_buf[(2 * k + 1) * Q:(2 * k + 2) * Q, :], spread, preferred_element_type=F32)
            scaled = (v_buf[k * Q:(k + 1) * Q, lanes].astype(F32) * grow).astype(BF16)
            both = jnp.dot(sb_buf[k], scaled, preferred_element_type=F32)
            d_buf[g, k * Q:(k + 1) * Q, :] = both[0:Q]
            state = rows[1 + blocks + k:2 + blocks + k] * state + rows[1 + k:2 + k] * both[Q:]
            l_buf[k, g] = state
        x_out[g, 0:state_dim, :] = state.astype(BF16)
        decay = rows[3 * blocks:3 * blocks + 1]
        high = decay.astype(BF16).astype(F32)
        tail = lax.broadcasted_iota(jnp.int32, (16, width), 0)
        x_out[g, state_dim:state_dim + 16, :] = jnp.where(
            tail == 0, high, jnp.where(tail == 1, decay - high, 0.0)).astype(BF16)
        x_copy(g).start()
        return carry

    ahead = min(4, chunks)
    lax.fori_loop(0, ahead, local_part, 0)

    def carried_part(g, carry):
        lanes = pl.ds(pl.multiple_of(g * width, width), width)
        rows = row_buf[g]
        x_copy(g).wait_recv()
        other = x_in[g, 0:state_dim, :].astype(F32)
        other_tail = x_in[g, state_dim:state_dim + 16, :].astype(F32)
        other_decay = other_tail[0:1] + other_tail[1:2]
        mine = l_buf[blocks - 1, g]
        mine_decay = rows[3 * blocks:3 * blocks + 1]
        is_second = second == 1
        first_state = jnp.where(is_second, other, mine)
        last_state = jnp.where(is_second, mine, other)
        first_decay = jnp.where(is_second, other_decay, mine_decay)
        last_decay = jnp.where(is_second, mine_decay, other_decay)

        @pl.when(rung > 0)
        def _():
            z_copy(g).wait_recv()

        enter = z_in[g].astype(F32)
        middle = first_decay * enter + first_state

        @pl.when(rung < rungs - 1)
        def _():
            z_out[g] = (last_decay * middle + last_state).astype(BF16)
            z_copy(g).start()

        enter = jnp.where(is_second, middle, enter)
        skip_lanes = rows[0:1]
        for k in range(blocks):
            span = slice(k * Q, (k + 1) * Q)
            at_block = enter
            if k > 0:
                at_block = rows[2 * blocks + k:2 * blocks + k + 1] * enter + l_buf[k - 1, g]
            scaled = (rows[1 + k:2 + k] * at_block).astype(BF16)
            inner = d_buf[g, span, :] + jnp.dot(
                c_ref[span, :], scaled, preferred_element_type=F32)
            o_buf[g, span, :] = (
                a_buf[g, span, :] * inner + skip_lanes * v_buf[span, lanes].astype(F32)
            ).astype(BF16)
        for j in range(len(far)):
            far_copy(j, g).start()
        twin_copy(g).start()
        own_copy(g).start()
        return carry

    def both_parts(g, carry):
        carried_part(g, 0)
        return local_part(g + ahead, carry)

    lax.fori_loop(0, chunks - ahead, both_parts, 0)
    lax.fori_loop(chunks - ahead, chunks, carried_part, 0)

    def forward(g, carry):
        for j in range(len(far)):
            far_copy(j, g).wait_recv()
            forward_copy(j, g).start()
        return carry

    lax.fori_loop(0, chunks, forward, 0)

    def finish(g, carry):
        x_copy(g).wait_send()

        @pl.when(rung < rungs - 1)
        def _():
            z_copy(g).wait_send()

        for j in range(len(far)):
            far_copy(j, g).wait_send()
            forward_copy(j, g).wait()
        twin_copy(g).wait()
        own_copy(g).wait()
        return carry

    lax.fori_loop(0, chunks, finish, 0)


def pick_kernel(blocks, owner, me, taken, out, zeros, held, load_sem, store_sem):
    chunks, width = taken.shape[1], taken.shape[3]
    slots = out.shape[1]
    zeros[...] = jnp.zeros_like(zeros)
    places = []
    for i in range(slots):
        doc, rank = i // CAP, i % CAP
        seen = jnp.int32(0)
        block = jnp.int32(0)
        present = jnp.bool_(False)
        for j in range(blocks):
            match = owner[j, doc] == me[0]
            hit = match & (seen == rank)
            block = jnp.where(hit, j, block)
            present = present | hit
            seen = seen + match.astype(jnp.int32)
        places.append(present)
        rows = pl.ds(pl.multiple_of(block * Q, Q), Q)

        @pl.when(present)
        def _():
            for g in range(chunks):
                pltpu.make_async_copy(
                    taken.at[doc, g, rows, :],
                    held.at[i, :, pl.ds(g * width, width)],
                    load_sem.at[i],
                ).start()

        @pl.when(jnp.logical_not(present))
        def _():
            pltpu.make_async_copy(zeros, out.at[0, i], store_sem.at[i]).start()

    for i, present in enumerate(places):
        @pl.when(present)
        def _():
            pltpu.make_async_copy(held.at[i], held.at[i], load_sem.at[i]).wait()
            pltpu.make_async_copy(held.at[i], out.at[0, i], store_sem.at[i]).start()

    for i in range(slots):
        pltpu.make_async_copy(zeros, out.at[0, i], store_sem.at[i]).wait()


def local(n_seq, n_doc, values, b_in, c_in, log_decay, skip, owner):
    seq_len, row_width = values.shape[1], values.shape[2]
    heads = log_decay.shape[1]
    state_dim = b_in.shape[2]
    blocks = seq_len // Q
    width = min(256, row_width)
    chunks = row_width // width
    far = n_doc // 2 - 1
    row_count = -(-(1 + 3 * blocks) // 16) * 16
    smem = pl.BlockSpec(memory_space=pltpu.SMEM)
    anywhere = pl.BlockSpec(memory_space=pl.ANY)
    dma = pltpu.SemaphoreType.DMA
    gathered = pl.pallas_call(
        functools.partial(layer_kernel, n_seq, n_doc, heads, width, chunks),
        out_shape=jax.ShapeDtypeStruct((n_doc, chunks, seq_len, width), BF16),
        in_specs=[anywhere] * 5,
        out_specs=anywhere,
        scratch_shapes=[
            pltpu.VMEM((seq_len, row_width), BF16),
            pltpu.VMEM((seq_len, state_dim), BF16),
            pltpu.VMEM((seq_len, state_dim), BF16),
            pltpu.VMEM((heads, seq_len), F32),
            pltpu.VMEM((1, heads), F32),
            pltpu.VMEM((2 * seq_len + row_count, 2 * heads), BF16),
            pltpu.VMEM((blocks, Q + state_dim, Q), BF16),
            pltpu.VMEM((chunks, seq_len, width), F32),
            pltpu.VMEM((chunks, seq_len, width), F32),
            pltpu.VMEM((chunks, row_count, width), F32),
            pltpu.VMEM((blocks, chunks, state_dim, width), F32),
            pltpu.VMEM((chunks, state_dim + 16, width), BF16),
            pltpu.VMEM((chunks, state_dim + 16, width), BF16),
            pltpu.VMEM((chunks, state_dim, width), BF16),
            pltpu.VMEM((chunks, state_dim, width), BF16),
            pltpu.VMEM((chunks, seq_len, width), BF16),
            dma((5,)),
            dma((chunks,)),
            dma((chunks,)),
            dma((chunks,)),
            dma((chunks,)),
            dma((chunks,)),
            dma((far, chunks)),
            dma((far, chunks)),
            dma((chunks,)),
            dma((chunks,)),
            dma((far, chunks)),
            dma((far, chunks)),
        ],
        compiler_params=pltpu.CompilerParams(
            collective_id=0, has_side_effects=True, vmem_limit_bytes=60 * 2**20
        ),
        name="layer",
    )(values[0], b_in[0], c_in[0], log_decay[0], skip.reshape(1, heads))

    slots = n_doc * CAP
    me = lax.axis_index("doc").astype(jnp.int32).reshape(1)

    return pl.pallas_call(
        functools.partial(pick_kernel, blocks),
        out_shape=jax.ShapeDtypeStruct((1, slots, Q, row_width), BF16),
        in_specs=[smem, smem, anywhere],
        out_specs=anywhere,
        scratch_shapes=[
            pltpu.VMEM((Q, row_width), BF16),
            pltpu.VMEM((slots, Q, row_width), BF16),
            dma((slots,)),
            dma((slots,)),
        ],
        compiler_params=pltpu.CompilerParams(vmem_limit_bytes=60 * 2**20),
        name="pick",
    )(owner.T, me, gathered)


def solution(mesh):
    in_specs = (
        P("doc", "seq", None),
        P("doc", "seq", None),
        P("doc", "seq", None),
        P("doc", None, "seq"),
        P(),
        P(None, "seq"),
    )
    out_specs = P("doc", "seq", None, None)
    body = functools.partial(local, mesh.shape["seq"], mesh.shape["doc"])
    return jax.shard_map(body, mesh=mesh, in_specs=in_specs, out_specs=out_specs, check_vma=False)
```

```python
import functools

import jax
import jax.numpy as jnp
from jax import lax
from jax.experimental import pallas as pl
from jax.experimental.pallas import tpu as pltpu
from jax.sharding import PartitionSpec as P

Q = 128
CAP = 2
MESH = pl.DeviceIdType.MESH
F32 = jnp.float32
BF16 = jnp.bfloat16


def layer_kernel(
    n_seq, n_doc, heads, width, chunks, group,
    v_hbm, b_hbm, c_hbm, ld_hbm, skip_hbm, gathered,
    v_buf, b_ref, c_ref, ld_ref, skip_ref, lhs_buf, sb_buf, a_buf, d_buf, row_buf, l_buf, x_out, x_in, z_out, z_in, o_buf,
    in_sem, own_sem, xs, xr, zs, zr, ys, yr, cs, cr, fs, fr,
):
    seq_len, row_width = v_buf.shape
    blocks = seq_len // Q
    state_dim = b_ref.shape[1]
    head_dim = row_width // heads
    sides = n_doc // 2
    rungs = n_seq // 2
    seq = lax.axis_index("seq")
    doc = lax.axis_index("doc")
    rung, second = seq // 2, seq % 2
    side, core = doc // 2, doc % 2
    across = (seq + 1 - 2 * second, doc)
    above = (seq + 2, doc)
    below = (seq - 2, doc)
    twin = (seq, doc + 1 - 2 * core)
    far = [(seq, ((side + j) % sides) * 2 + core) for j in range(1, sides)]

    pairs = [(ld_hbm, ld_ref), (skip_hbm, skip_ref), (b_hbm, b_ref), (c_hbm, c_ref), (v_hbm, v_buf)]
    loads = [pltpu.make_async_copy(a, b, in_sem.at[i]) for i, (a, b) in enumerate(pairs)]
    for load in loads:
        load.start()

    barrier = pltpu.get_barrier_semaphore()
    for other in [across, twin] + far:
        pl.semaphore_signal(barrier, inc=1, device_id=other, device_id_type=MESH)

    @pl.when(rung > 0)
    def _():
        pl.semaphore_signal(barrier, inc=1, device_id=below, device_id_type=MESH)

    @pl.when(rung < rungs - 1)
    def _():
        pl.semaphore_signal(barrier, inc=1, device_id=above, device_id_type=MESH)

    for load in loads[:-1]:
        load.wait()

    rows_i = lax.broadcasted_iota(jnp.int32, (Q, Q), 0)
    cols_i = lax.broadcasted_iota(jnp.int32, (Q, Q), 1)
    lower = rows_i >= cols_i
    ones_lower = jnp.where(lower, 1.0, 0.0).astype(F32)
    lane = lax.broadcasted_iota(jnp.int32, (1, 2 * heads), 1)
    twice = (
        lax.broadcasted_iota(jnp.int32, (heads, 2 * heads), 1) % heads
        == lax.broadcasted_iota(jnp.int32, (heads, 2 * heads), 0)
    )
    skip_row = jnp.dot(
        jnp.broadcast_to(skip_ref[...], (8, heads)), jnp.where(twice, 1.0, 0.0).astype(F32),
        precision=lax.Precision.HIGHEST, preferred_element_type=F32,
    )[0:1]

    def split(x):
        high = x.astype(BF16).astype(F32)
        return jnp.where(lane < heads, high, x - high).astype(BF16)

    small = [skip_row]
    halves, totals, befores = [], [], []
    running = jnp.zeros((1, 2 * heads), F32)
    for k in range(blocks):
        span = slice(k * Q, (k + 1) * Q)
        decay = ld_ref[:, span]
        decay = jnp.concatenate([decay, decay], axis=0)
        cum = lax.dot_general(
            ones_lower, decay, (((1,), (1,)), ((), ())),
            precision=lax.Precision.HIGHEST, preferred_element_type=F32,
        )
        total = cum[Q - 1:Q]
        half = 0.5 * total
        lhs_buf[2 * k * Q:(2 * k + 1) * Q, :] = split(jnp.exp(cum - half))
        lhs_buf[(2 * k + 1) * Q:(2 * k + 2) * Q, :] = split(jnp.exp(half - cum))
        running = running + total
        halves.append(jnp.exp(half))
        totals.append(jnp.exp(total))
        befores.append(jnp.exp(running))
        b_block = b_ref[span, :]
        scores = lax.dot_general(
            c_ref[span, :], b_block, (((1,), (1,)), ((), ())), preferred_element_type=F32
        )
        sb_buf[k, 0:Q, :] = jnp.where(lower, scores, 0.0).astype(BF16)
        sb_buf[k, Q:Q + state_dim, :] = b_block.astype(F32).T.astype(BF16)
    small = [skip_row] + halves + totals + befores
    row_count = row_buf.shape[1]
    row_id = lax.broadcasted_iota(jnp.int32, (row_count, 2 * heads), 0)
    stacked = jnp.zeros((row_count, 2 * heads), F32)
    for i, row in enumerate(small):
        stacked = jnp.where(row_id == i, row, stacked)
    base = 2 * blocks * Q
    lhs_buf[base:base + row_count, :] = split(stacked)

    @pl.when(rung == 0)
    def _():
        z_in[...] = jnp.zeros_like(z_in)

    peers = 2 + len(far) + jnp.where(rung > 0, 1, 0) + jnp.where(rung < rungs - 1, 1, 0)
    pl.semaphore_wait(barrier, peers)
    loads[-1].wait()

    def x_copy(g):
        return pltpu.make_async_remote_copy(
            x_out.at[g], x_in.at[g], xs.at[g], xr.at[g], device_id=across, device_id_type=MESH)

    def z_copy(g):
        return pltpu.make_async_remote_copy(
            z_out.at[g], z_in.at[g], zs.at[g], zr.at[g], device_id=above, device_id_type=MESH)

    def far_copy(j, g):
        return pltpu.make_async_remote_copy(
            o_buf.at[g], gathered.at[doc, g], ys.at[j, g], yr.at[j, g],
            device_id=far[j], device_id_type=MESH)

    def twin_copy(g):
        return pltpu.make_async_remote_copy(
            o_buf.at[g], gathered.at[doc, g], cs.at[g], cr.at[g],
            device_id=twin, device_id_type=MESH)

    def own_copy(g):
        return pltpu.make_async_copy(o_buf.at[g], gathered.at[doc, g], own_sem.at[g])

    def forward_copy(j, g):
        source = ((side + sides - 1 - j) % sides) * 2 + core
        return pltpu.make_async_remote_copy(
            gathered.at[source, g], gathered.at[source, g], fs.at[j, g], fr.at[j, g],
            device_id=twin, device_id_type=MESH)

    def local_part(g, carry):
        lanes = pl.ds(pl.multiple_of(g * width, width), width)
        head_of = lax.broadcasted_iota(jnp.int32, (2 * heads, width), 1) // head_dim
        head_at = lax.broadcasted_iota(jnp.int32, (2 * heads, width), 0) % heads
        spread = jnp.where(head_at == head_of + g * (width // head_dim), 1.0, 0.0).astype(BF16)
        rows = jnp.dot(lhs_buf[base:base + row_count, :], spread, preferred_element_type=F32)
        row_buf[g] = rows
        state = jnp.zeros((state_dim, width), F32)
        for k in range(blocks):
            a_buf[g, k * Q:(k + 1) * Q, :] = jnp.dot(
                lhs_buf[2 * k * Q:(2 * k + 1) * Q, :], spread, preferred_element_type=F32)
            grow = jnp.dot(
                lhs_buf[(2 * k + 1) * Q:(2 * k + 2) * Q, :], spread, preferred_element_type=F32)
            scaled = (v_buf[k * Q:(k + 1) * Q, lanes].astype(F32) * grow).astype(BF16)
            both = jnp.dot(sb_buf[k], scaled, preferred_element_type=F32)
            d_buf[g, k * Q:(k + 1) * Q, :] = both[0:Q]
            state = rows[1 + blocks + k:2 + blocks + k] * state + rows[1 + k:2 + k] * both[Q:]
            l_buf[k, g] = state
        x_out[g, 0:state_dim, :] = state.astype(BF16)
        decay = rows[3 * blocks:3 * blocks + 1]
        high = decay.astype(BF16).astype(F32)
        tail = lax.broadcasted_iota(jnp.int32, (16, width), 0)
        x_out[g, state_dim:state_dim + 16, :] = jnp.where(
            tail == 0, high, jnp.where(tail == 1, decay - high, 0.0)).astype(BF16)
        x_copy(g).start()
        return carry

    ahead = min(2, chunks // group)
    lax.fori_loop(0, ahead * group, local_part, 0)

    def carried_part(step, part):
        g = step * group + part
        lanes = pl.ds(pl.multiple_of(g * width, width), width)
        o_lanes = pl.ds(part * width, width)
        rows = row_buf[g]
        x_copy(g).wait_recv()
        other = x_in[g, 0:state_dim, :].astype(F32)
        other_tail = x_in[g, state_dim:state_dim + 16, :].astype(F32)
        other_decay = other_tail[0:1] + other_tail[1:2]
        mine = l_buf[blocks - 1, g]
        mine_decay = rows[3 * blocks:3 * blocks + 1]
        is_second = second == 1
        first_state = jnp.where(is_second, other, mine)
        last_state = jnp.where(is_second, mine, other)
        first_decay = jnp.where(is_second, other_decay, mine_decay)
        last_decay = jnp.where(is_second, mine_decay, other_decay)

        @pl.when(rung > 0)
        def _():
            z_copy(g).wait_recv()

        enter = z_in[g].astype(F32)
        middle = first_decay * enter + first_state

        @pl.when(rung < rungs - 1)
        def _():
            z_out[g] = (last_decay * middle + last_state).astype(BF16)
            z_copy(g).start()

        enter = jnp.where(is_second, middle, enter)
        skip_lanes = rows[0:1]
        for k in range(blocks):
            span = slice(k * Q, (k + 1) * Q)
            at_block = enter
            if k > 0:
                at_block = rows[2 * blocks + k:2 * blocks + k + 1] * enter + l_buf[k - 1, g]
            scaled = (rows[1 + k:2 + k] * at_block).astype(BF16)
            inner = d_buf[g, span, :] + jnp.dot(
                c_ref[span, :], scaled, preferred_element_type=F32)
            o_buf[g // group, span, o_lanes] = (
                a_buf[g, span, :] * inner + skip_lanes * v_buf[span, lanes].astype(F32)
            ).astype(BF16)

    def send(step):
        for j in range(len(far)):
            far_copy(j, step).start()
        twin_copy(step).start()
        own_copy(step).start()

    def outputs(step, carry):
        for part in range(group):
            carried_part(step, part)
        send(step)
        return carry

    def outputs_and_later(step, carry):
        outputs(step, carry)
        for part in range(group):
            local_part((step + ahead) * group + part, carry)
        return carry

    steps = chunks // group
    lax.fori_loop(0, steps - ahead, outputs_and_later, 0)
    lax.fori_loop(steps - ahead, steps, outputs, 0)

    def forward(g, carry):
        for j in range(len(far)):
            far_copy(j, g).wait_recv()
            forward_copy(j, g).start()
        return carry

    lax.fori_loop(0, steps, forward, 0)

    def finish(g, carry):
        for j in range(len(far)):
            far_copy(j, g).wait_send()
            forward_copy(j, g).wait()
        twin_copy(g).wait()
        own_copy(g).wait()
        return carry

    lax.fori_loop(0, steps, finish, 0)

    def finish_states(g, carry):
        x_copy(g).wait_send()

        @pl.when(rung < rungs - 1)
        def _():
            z_copy(g).wait_send()

        return carry

    lax.fori_loop(0, chunks, finish_states, 0)


def pick_kernel(blocks, owner, me, taken, out, zeros, store_sem):
    chunks, width = taken.shape[1], taken.shape[3]
    slots = out.shape[1]
    zeros[...] = jnp.zeros_like(zeros)
    for i in range(slots):
        doc, rank = i // CAP, i % CAP
        seen = jnp.int32(0)
        block = jnp.int32(0)
        present = jnp.bool_(False)
        for j in range(blocks):
            match = owner[j, doc] == me[0]
            hit = match & (seen == rank)
            block = jnp.where(hit, j, block)
            present = present | hit
            seen = seen + match.astype(jnp.int32)
        rows = pl.ds(pl.multiple_of(block * Q, Q), Q)

        @pl.when(present)
        def _():
            for g in range(chunks):
                pltpu.make_async_copy(
                    taken.at[doc, g, rows, :],
                    out.at[0, i, :, pl.ds(g * width, width)],
                    store_sem.at[i],
                ).start()

        @pl.when(jnp.logical_not(present))
        def _():
            pltpu.make_async_copy(zeros, out.at[0, i], store_sem.at[i]).start()

    for i in range(slots):
        pltpu.make_async_copy(zeros, out.at[0, i], store_sem.at[i]).wait()


def local(n_seq, n_doc, values, b_in, c_in, log_decay, skip, owner):
    seq_len, row_width = values.shape[1], values.shape[2]
    heads = log_decay.shape[1]
    state_dim = b_in.shape[2]
    blocks = seq_len // Q
    group = 2
    width = 128
    chunks = row_width // width
    steps, step_width = chunks // group, width * group
    far = n_doc // 2 - 1
    row_count = -(-(1 + 3 * blocks) // 16) * 16
    smem = pl.BlockSpec(memory_space=pltpu.SMEM)
    anywhere = pl.BlockSpec(memory_space=pl.ANY)
    dma = pltpu.SemaphoreType.DMA
    gathered = pl.pallas_call(
        functools.partial(layer_kernel, n_seq, n_doc, heads, width, chunks, group),
        out_shape=jax.ShapeDtypeStruct((n_doc, steps, seq_len, step_width), BF16),
        in_specs=[anywhere] * 5,
        out_specs=anywhere,
        scratch_shapes=[
            pltpu.VMEM((seq_len, row_width), BF16),
            pltpu.VMEM((seq_len, state_dim), BF16),
            pltpu.VMEM((seq_len, state_dim), BF16),
            pltpu.VMEM((heads, seq_len), F32),
            pltpu.VMEM((1, heads), F32),
            pltpu.VMEM((2 * seq_len + row_count, 2 * heads), BF16),
            pltpu.VMEM((blocks, Q + state_dim, Q), BF16),
            pltpu.VMEM((chunks, seq_len, width), F32),
            pltpu.VMEM((chunks, seq_len, width), F32),
            pltpu.VMEM((chunks, row_count, width), F32),
            pltpu.VMEM((blocks, chunks, state_dim, width), F32),
            pltpu.VMEM((chunks, state_dim + 16, width), BF16),
            pltpu.VMEM((chunks, state_dim + 16, width), BF16),
            pltpu.VMEM((chunks, state_dim, width), BF16),
            pltpu.VMEM((chunks, state_dim, width), BF16),
            pltpu.VMEM((steps, seq_len, step_width), BF16),
            dma((5,)),
            dma((steps,)),
            dma((chunks,)),
            dma((chunks,)),
            dma((chunks,)),
            dma((chunks,)),
            dma((far, steps)),
            dma((far, steps)),
            dma((steps,)),
            dma((steps,)),
            dma((far, steps)),
            dma((far, steps)),
        ],
        compiler_params=pltpu.CompilerParams(
            collective_id=0, has_side_effects=True, vmem_limit_bytes=60 * 2**20
        ),
        name="layer",
    )(values[0], b_in[0], c_in[0], log_decay[0], skip.reshape(1, heads))

    slots = n_doc * CAP
    me = lax.axis_index("doc").astype(jnp.int32).reshape(1)

    return pl.pallas_call(
        functools.partial(pick_kernel, blocks),
        out_shape=jax.ShapeDtypeStruct((1, slots, Q, row_width), BF16),
        in_specs=[smem, smem, anywhere],
        out_specs=anywhere,
        scratch_shapes=[
            pltpu.VMEM((Q, row_width), BF16),
            dma((slots,)),
        ],
        compiler_params=pltpu.CompilerParams(vmem_limit_bytes=60 * 2**20),
        name="pick",
    )(owner.T, me, gathered)


def solution(mesh):
    in_specs = (
        P("doc", "seq", None),
        P("doc", "seq", None),
        P("doc", "seq", None),
        P("doc", None, "seq"),
        P(),
        P(None, "seq"),
    )
    out_specs = P("doc", "seq", None, None)
    body = functools.partial(local, mesh.shape["seq"], mesh.shape["doc"])
    return jax.shard_map(body, mesh=mesh, in_specs=in_specs, out_specs=out_specs, check_vma=False)
```

```python
import functools

import jax
import jax.numpy as jnp
from jax import lax
from jax.experimental import pallas as pl
from jax.experimental.pallas import tpu as pltpu
from jax.sharding import PartitionSpec as P

Q = 128
CAP = 2
MESH = pl.DeviceIdType.MESH
F32 = jnp.float32
BF16 = jnp.bfloat16


def layer_kernel(
    n_seq, n_doc, heads, width, chunks, group,
    v_hbm, b_hbm, c_hbm, ld_hbm, skip_hbm, gathered,
    v_buf, b_ref, c_ref, ld_ref, skip_ref, lhs_buf, sb_buf, a_buf, d_buf, row_buf, l_buf, x_out, x_in, p_out, p_in, e_out, e_in, o_buf,
    in_sem, own_sem, xs, xr, ps, pr, es, e2s, er, ys, yr, cs, cr, fs, fr,
):
    seq_len, row_width = v_buf.shape
    blocks = seq_len // Q
    state_dim = b_ref.shape[1]
    head_dim = row_width // heads
    sides = n_doc // 2
    rungs = n_seq // 2
    seq = lax.axis_index("seq")
    doc = lax.axis_index("doc")
    rung, second = seq // 2, seq % 2
    side, core = doc // 2, doc % 2
    across = (seq + 1 - 2 * second, doc)
    above = (seq + 2, doc)
    below = (seq - 2, doc)
    above2 = (seq + 4, doc)
    below2 = (seq - 4, doc)
    odd = rung % 2 == 1
    has_above = rung < rungs - 1
    sends_p = jnp.logical_not(odd) & has_above
    sends_e = odd & has_above
    sends_e2 = odd & (rung < rungs - 2)
    takes_e = rung > 1
    from_below2 = odd & takes_e
    twin = (seq, doc + 1 - 2 * core)
    far = [(seq, ((side + j) % sides) * 2 + core) for j in range(1, sides)]

    pairs = [(ld_hbm, ld_ref), (skip_hbm, skip_ref), (b_hbm, b_ref), (c_hbm, c_ref), (v_hbm, v_buf)]
    loads = [pltpu.make_async_copy(a, b, in_sem.at[i]) for i, (a, b) in enumerate(pairs)]
    for load in loads:
        load.start()

    barrier = pltpu.get_barrier_semaphore()
    for other in [across, twin] + far:
        pl.semaphore_signal(barrier, inc=1, device_id=other, device_id_type=MESH)

    @pl.when(rung > 0)
    def _():
        pl.semaphore_signal(barrier, inc=1, device_id=below, device_id_type=MESH)

    @pl.when(has_above)
    def _():
        pl.semaphore_signal(barrier, inc=1, device_id=above, device_id_type=MESH)

    @pl.when(sends_e2)
    def _():
        pl.semaphore_signal(barrier, inc=1, device_id=above2, device_id_type=MESH)

    @pl.when(from_below2)
    def _():
        pl.semaphore_signal(barrier, inc=1, device_id=below2, device_id_type=MESH)

    for load in loads[:-1]:
        load.wait()

    rows_i = lax.broadcasted_iota(jnp.int32, (Q, Q), 0)
    cols_i = lax.broadcasted_iota(jnp.int32, (Q, Q), 1)
    lower = rows_i >= cols_i
    ones_lower = jnp.where(lower, 1.0, 0.0).astype(F32)
    lane = lax.broadcasted_iota(jnp.int32, (1, 2 * heads), 1)
    twice = (
        lax.broadcasted_iota(jnp.int32, (heads, 2 * heads), 1) % heads
        == lax.broadcasted_iota(jnp.int32, (heads, 2 * heads), 0)
    )
    skip_row = jnp.dot(
        jnp.broadcast_to(skip_ref[...], (8, heads)), jnp.where(twice, 1.0, 0.0).astype(F32),
        precision=lax.Precision.HIGHEST, preferred_element_type=F32,
    )[0:1]

    def split(x):
        high = x.astype(BF16).astype(F32)
        return jnp.where(lane < heads, high, x - high).astype(BF16)

    small = [skip_row]
    halves, totals, befores = [], [], []
    running = jnp.zeros((1, 2 * heads), F32)
    for k in range(blocks):
        span = slice(k * Q, (k + 1) * Q)
        decay = ld_ref[:, span]
        decay = jnp.concatenate([decay, decay], axis=0)
        cum = lax.dot_general(
            ones_lower, decay, (((1,), (1,)), ((), ())),
            precision=lax.Precision.HIGHEST, preferred_element_type=F32,
        )
        total = cum[Q - 1:Q]
        half = 0.5 * total
        lhs_buf[2 * k * Q:(2 * k + 1) * Q, :] = split(jnp.exp(cum - half))
        lhs_buf[(2 * k + 1) * Q:(2 * k + 2) * Q, :] = split(jnp.exp(half - cum))
        running = running + total
        halves.append(jnp.exp(half))
        totals.append(jnp.exp(total))
        befores.append(jnp.exp(running))
        b_block = b_ref[span, :]
        scores = lax.dot_general(
            c_ref[span, :], b_block, (((1,), (1,)), ((), ())), preferred_element_type=F32
        )
        sb_buf[k, 0:Q, :] = jnp.where(lower, scores, 0.0).astype(BF16)
        sb_buf[k, Q:Q + state_dim, :] = b_block.astype(F32).T.astype(BF16)
    small = [skip_row] + halves + totals + befores
    row_count = row_buf.shape[1]
    row_id = lax.broadcasted_iota(jnp.int32, (row_count, 2 * heads), 0)
    stacked = jnp.zeros((row_count, 2 * heads), F32)
    for i, row in enumerate(small):
        stacked = jnp.where(row_id == i, row, stacked)
    base = 2 * blocks * Q
    lhs_buf[base:base + row_count, :] = split(stacked)

    @pl.when(jnp.logical_not(takes_e))
    def _():
        e_in[...] = jnp.zeros_like(e_in)

    @pl.when(jnp.logical_not(odd))
    def _():
        p_in[...] = jnp.zeros_like(p_in)

    peers = 2 + len(far) + jnp.where(rung > 0, 1, 0) + jnp.where(has_above, 1, 0)
    peers = peers + jnp.where(sends_e2, 1, 0) + jnp.where(from_below2, 1, 0)
    pl.semaphore_wait(barrier, peers)
    loads[-1].wait()

    def x_copy(g):
        return pltpu.make_async_remote_copy(
            x_out.at[g], x_in.at[g], xs.at[g], xr.at[g], device_id=across, device_id_type=MESH)

    def p_copy(g):
        return pltpu.make_async_remote_copy(
            p_out.at[g], p_in.at[g], ps.at[g], pr.at[g], device_id=above, device_id_type=MESH)

    def e_copy(g):
        return pltpu.make_async_remote_copy(
            e_out.at[g], e_in.at[g], es.at[g], er.at[g], device_id=above, device_id_type=MESH)

    def e2_copy(g):
        return pltpu.make_async_remote_copy(
            e_out.at[g], e_in.at[g], e2s.at[g], er.at[g], device_id=above2, device_id_type=MESH)

    def with_decay(buf, g, state, decay):
        high = decay.astype(BF16).astype(F32)
        tail = lax.broadcasted_iota(jnp.int32, (16, width), 0)
        buf[g, 0:state_dim, :] = state.astype(BF16)
        buf[g, state_dim:state_dim + 16, :] = jnp.where(
            tail == 0, high, jnp.where(tail == 1, decay - high, 0.0)).astype(BF16)

    def without_decay(buf, g):
        tail = buf[g, state_dim:state_dim + 16, :].astype(F32)
        return buf[g, 0:state_dim, :].astype(F32), tail[0:1] + tail[1:2]

    def far_copy(j, g):
        return pltpu.make_async_remote_copy(
            o_buf.at[g], gathered.at[doc, g], ys.at[j, g], yr.at[j, g],
            device_id=far[j], device_id_type=MESH)

    def twin_copy(g):
        return pltpu.make_async_remote_copy(
            o_buf.at[g], gathered.at[doc, g], cs.at[g], cr.at[g],
            device_id=twin, device_id_type=MESH)

    def own_copy(g):
        return pltpu.make_async_copy(o_buf.at[g], gathered.at[doc, g], own_sem.at[g])

    def forward_copy(j, g):
        source = ((side + sides - 1 - j) % sides) * 2 + core
        return pltpu.make_async_remote_copy(
            gathered.at[source, g], gathered.at[source, g], fs.at[j, g], fr.at[j, g],
            device_id=twin, device_id_type=MESH)

    def local_part(g, carry):
        lanes = pl.ds(pl.multiple_of(g * width, width), width)
        head_of = lax.broadcasted_iota(jnp.int32, (2 * heads, width), 1) // head_dim
        head_at = lax.broadcasted_iota(jnp.int32, (2 * heads, width), 0) % heads
        spread = jnp.where(head_at == head_of + g * (width // head_dim), 1.0, 0.0).astype(BF16)
        rows = jnp.dot(lhs_buf[base:base + row_count, :], spread, preferred_element_type=F32)
        row_buf[g] = rows
        state = jnp.zeros((state_dim, width), F32)
        for k in range(blocks):
            a_buf[g, k * Q:(k + 1) * Q, :] = jnp.dot(
                lhs_buf[2 * k * Q:(2 * k + 1) * Q, :], spread, preferred_element_type=F32)
            grow = jnp.dot(
                lhs_buf[(2 * k + 1) * Q:(2 * k + 2) * Q, :], spread, preferred_element_type=F32)
            scaled = (v_buf[k * Q:(k + 1) * Q, lanes].astype(F32) * grow).astype(BF16)
            both = jnp.dot(sb_buf[k], scaled, preferred_element_type=F32)
            d_buf[g, k * Q:(k + 1) * Q, :] = both[0:Q]
            state = rows[1 + blocks + k:2 + blocks + k] * state + rows[1 + k:2 + k] * both[Q:]
            l_buf[k, g] = state
        with_decay(x_out, g, state, rows[3 * blocks:3 * blocks + 1])
        x_copy(g).start()
        return carry

    ahead = min(2, chunks // group)
    lax.fori_loop(0, ahead * group, local_part, 0)

    def carried_part(step, part):
        g = step * group + part
        lanes = pl.ds(pl.multiple_of(g * width, width), width)
        o_lanes = pl.ds(part * width, width)
        rows = row_buf[g]
        x_copy(g).wait_recv()
        other, other_decay = without_decay(x_in, g)
        mine = l_buf[blocks - 1, g]
        mine_decay = rows[3 * blocks:3 * blocks + 1]
        is_second = second == 1
        first_state = jnp.where(is_second, other, mine)
        last_state = jnp.where(is_second, mine, other)
        first_decay = jnp.where(is_second, other_decay, mine_decay)
        last_decay = jnp.where(is_second, mine_decay, other_decay)

        @pl.when(sends_p)
        def _():
            with_decay(p_out, g, last_decay * first_state + last_state, first_decay * last_decay)
            p_copy(g).start()

        @pl.when(odd)
        def _():
            p_copy(g).wait_recv()

        @pl.when(takes_e)
        def _():
            e_copy(g).wait_recv()

        past = e_in[g].astype(F32)
        under, under_decay = without_decay(p_in, g)
        enter = jnp.where(odd, under_decay * past + under, past)
        middle = first_decay * enter + first_state

        @pl.when(sends_e)
        def _():
            e_out[g] = (last_decay * middle + last_state).astype(BF16)

        @pl.when(sends_e2)
        def _():
            e2_copy(g).start()

        @pl.when(sends_e)
        def _():
            e_copy(g).start()

        enter = jnp.where(is_second, middle, enter)
        skip_lanes = rows[0:1]
        for k in range(blocks):
            span = slice(k * Q, (k + 1) * Q)
            at_block = enter
            if k > 0:
                at_block = rows[2 * blocks + k:2 * blocks + k + 1] * enter + l_buf[k - 1, g]
            scaled = (rows[1 + k:2 + k] * at_block).astype(BF16)
            inner = d_buf[g, span, :] + jnp.dot(
                c_ref[span, :], scaled, preferred_element_type=F32)
            o_buf[g // group, span, o_lanes] = (
                a_buf[g, span, :] * inner + skip_lanes * v_buf[span, lanes].astype(F32)
            ).astype(BF16)

    def send(step):
        for j in range(len(far)):
            far_copy(j, step).start()
        twin_copy(step).start()
        own_copy(step).start()

    def outputs(step, carry):
        for part in range(group):
            carried_part(step, part)
        send(step)
        return carry

    def outputs_and_later(step, carry):
        outputs(step, carry)
        for part in range(group):
            local_part((step + ahead) * group + part, carry)
        return carry

    steps = chunks // group
    lax.fori_loop(0, steps - ahead, outputs_and_later, 0)
    lax.fori_loop(steps - ahead, steps, outputs, 0)

    def forward(g, carry):
        for j in range(len(far)):
            far_copy(j, g).wait_recv()
            forward_copy(j, g).start()
        return carry

    lax.fori_loop(0, steps, forward, 0)

    def finish(g, carry):
        for j in range(len(far)):
            far_copy(j, g).wait_send()
            forward_copy(j, g).wait()
        twin_copy(g).wait()
        own_copy(g).wait()
        return carry

    lax.fori_loop(0, steps, finish, 0)

    def finish_states(g, carry):
        x_copy(g).wait_send()

        @pl.when(sends_p)
        def _():
            p_copy(g).wait_send()

        @pl.when(sends_e)
        def _():
            e_copy(g).wait_send()

        @pl.when(sends_e2)
        def _():
            e2_copy(g).wait_send()

        return carry

    lax.fori_loop(0, chunks, finish_states, 0)


def pick_kernel(blocks, owner, me, taken, out, zeros, held, flat, load_sem, store_sem):
    chunks, width = taken.shape[1], taken.shape[3]
    slots = out.shape[1]
    places = []
    for i in range(slots):
        doc, rank = i // CAP, i % CAP
        seen = jnp.int32(0)
        block = jnp.int32(0)
        present = jnp.bool_(False)
        for j in range(blocks):
            match = owner[j, doc] == me[0]
            hit = match & (seen == rank)
            block = jnp.where(hit, j, block)
            present = present | hit
            seen = seen + match.astype(jnp.int32)
        places.append(present)
        rows = pl.ds(pl.multiple_of(block * Q, Q), Q)

        @pl.when(present)
        def _():
            pltpu.make_async_copy(
                taken.at[doc, :, rows, :], held.at[i], load_sem.at[i]
            ).start()

    zeros[...] = jnp.zeros_like(zeros)
    for i, present in enumerate(places):

        @pl.when(jnp.logical_not(present))
        def _():
            pltpu.make_async_copy(zeros, out.at[0, i], store_sem.at[i]).start()

    for i, present in enumerate(places):

        @pl.when(present)
        def _():
            pltpu.make_async_copy(held.at[i], held.at[i], load_sem.at[i]).wait()

            def relay(g, carry):
                flat[i, :, pl.ds(pl.multiple_of(g * width, width), width)] = held[i, g]
                return carry

            lax.fori_loop(0, chunks, relay, 0)
            pltpu.make_async_copy(flat.at[i], out.at[0, i], store_sem.at[i]).start()

    for i in range(slots):
        pltpu.make_async_copy(zeros, out.at[0, i], store_sem.at[i]).wait()


def local(n_seq, n_doc, values, b_in, c_in, log_decay, skip, owner):
    seq_len, row_width = values.shape[1], values.shape[2]
    heads = log_decay.shape[1]
    state_dim = b_in.shape[2]
    blocks = seq_len // Q
    group = 2
    width = 128
    chunks = row_width // width
    steps, step_width = chunks // group, width * group
    far = n_doc // 2 - 1
    row_count = -(-(1 + 3 * blocks) // 16) * 16
    smem = pl.BlockSpec(memory_space=pltpu.SMEM)
    anywhere = pl.BlockSpec(memory_space=pl.ANY)
    dma = pltpu.SemaphoreType.DMA
    gathered = pl.pallas_call(
        functools.partial(layer_kernel, n_seq, n_doc, heads, width, chunks, group),
        out_shape=jax.ShapeDtypeStruct((n_doc, steps, seq_len, step_width), BF16),
        in_specs=[anywhere] * 5,
        out_specs=anywhere,
        scratch_shapes=[
            pltpu.VMEM((seq_len, row_width), BF16),
            pltpu.VMEM((seq_len, state_dim), BF16),
            pltpu.VMEM((seq_len, state_dim), BF16),
            pltpu.VMEM((heads, seq_len), F32),
            pltpu.VMEM((1, heads), F32),
            pltpu.VMEM((2 * seq_len + row_count, 2 * heads), BF16),
            pltpu.VMEM((blocks, Q + state_dim, Q), BF16),
            pltpu.VMEM((chunks, seq_len, width), F32),
            pltpu.VMEM((chunks, seq_len, width), F32),
            pltpu.VMEM((chunks, row_count, width), F32),
            pltpu.VMEM((blocks, chunks, state_dim, width), F32),
            pltpu.VMEM((chunks, state_dim + 16, width), BF16),
            pltpu.VMEM((chunks, state_dim + 16, width), BF16),
            pltpu.VMEM((chunks, state_dim + 16, width), BF16),
            pltpu.VMEM((chunks, state_dim + 16, width), BF16),
            pltpu.VMEM((chunks, state_dim, width), BF16),
            pltpu.VMEM((chunks, state_dim, width), BF16),
            pltpu.VMEM((steps, seq_len, step_width), BF16),
            dma((5,)),
            dma((steps,)),
            dma((chunks,)),
            dma((chunks,)),
            dma((chunks,)),
            dma((chunks,)),
            dma((chunks,)),
            dma((chunks,)),
            dma((chunks,)),
            dma((far, steps)),
            dma((far, steps)),
            dma((steps,)),
            dma((steps,)),
            dma((far, steps)),
            dma((far, steps)),
        ],
        compiler_params=pltpu.CompilerParams(
            collective_id=0, has_side_effects=True, vmem_limit_bytes=60 * 2**20
        ),
        name="layer",
    )(values[0], b_in[0], c_in[0], log_decay[0], skip.reshape(1, heads))

    slots = n_doc * CAP
    me = lax.axis_index("doc").astype(jnp.int32).reshape(1)

    return pl.pallas_call(
        functools.partial(pick_kernel, blocks),
        out_shape=jax.ShapeDtypeStruct((1, slots, Q, row_width), BF16),
        in_specs=[smem, smem, anywhere],
        out_specs=anywhere,
        scratch_shapes=[
            pltpu.VMEM((Q, row_width), BF16),
            pltpu.VMEM((slots, steps, Q, step_width), BF16),
            pltpu.VMEM((slots, Q, row_width), BF16),
            dma((slots,)),
            dma((slots,)),
        ],
        compiler_params=pltpu.CompilerParams(vmem_limit_bytes=60 * 2**20),
        name="pick",
    )(owner.T, me, gathered)


def solution(mesh):
    in_specs = (
        P("doc", "seq", None),
        P("doc", "seq", None),
        P("doc", "seq", None),
        P("doc", None, "seq"),
        P(),
        P(None, "seq"),
    )
    out_specs = P("doc", "seq", None, None)
    body = functools.partial(local, mesh.shape["seq"], mesh.shape["doc"])
    return jax.shard_map(body, mesh=mesh, in_specs=in_specs, out_specs=out_specs, check_vma=False)
```

```python
import functools

import jax
import jax.numpy as jnp
from jax import lax
from jax.experimental import pallas as pl
from jax.experimental.pallas import tpu as pltpu
from jax.sharding import PartitionSpec as P

Q = 128
CAP = 2
MESH = pl.DeviceIdType.MESH
F32 = jnp.float32
BF16 = jnp.bfloat16


def layer_kernel(
    n_seq, n_doc, heads, width, chunks, group,
    v_hbm, b_hbm, c_hbm, ld_hbm, skip_hbm, gathered,
    v_buf, b_ref, c_ref, ld_ref, skip_ref, lhs_buf, sb_buf, a_buf, d_buf, row_buf, l_buf, x_out, x_in, z_out, z_in, o_buf,
    in_sem, own_sem, xs, xr, zs, zr, ys, yr, cs, cr, fs, fr,
):
    seq_len, row_width = v_buf.shape
    blocks = seq_len // Q
    state_dim = b_ref.shape[1]
    head_dim = row_width // heads
    sides = n_doc // 2
    rungs = n_seq // 2
    seq = lax.axis_index("seq")
    doc = lax.axis_index("doc")
    rung, second = seq // 2, seq % 2
    side, core = doc // 2, doc % 2
    across = (seq + 1 - 2 * second, doc)
    above = (seq + 2, doc)
    below = (seq - 2, doc)
    twin = (seq, doc + 1 - 2 * core)
    far = [(seq, ((side + j) % sides) * 2 + core) for j in range(1, sides)]

    pairs = [(ld_hbm, ld_ref), (skip_hbm, skip_ref), (b_hbm, b_ref), (c_hbm, c_ref), (v_hbm, v_buf)]
    loads = [pltpu.make_async_copy(a, b, in_sem.at[i]) for i, (a, b) in enumerate(pairs)]
    for load in loads:
        load.start()

    barrier = pltpu.get_barrier_semaphore()
    for other in [across, twin] + far:
        pl.semaphore_signal(barrier, inc=1, device_id=other, device_id_type=MESH)

    @pl.when(rung > 0)
    def _():
        pl.semaphore_signal(barrier, inc=1, device_id=below, device_id_type=MESH)

    @pl.when(rung < rungs - 1)
    def _():
        pl.semaphore_signal(barrier, inc=1, device_id=above, device_id_type=MESH)

    for load in loads[:-1]:
        load.wait()

    rows_i = lax.broadcasted_iota(jnp.int32, (Q, Q), 0)
    cols_i = lax.broadcasted_iota(jnp.int32, (Q, Q), 1)
    lower = rows_i >= cols_i
    ones_lower = jnp.where(lower, 1.0, 0.0).astype(F32)
    lane = lax.broadcasted_iota(jnp.int32, (1, 2 * heads), 1)
    twice = (
        lax.broadcasted_iota(jnp.int32, (heads, 2 * heads), 1) % heads
        == lax.broadcasted_iota(jnp.int32, (heads, 2 * heads), 0)
    )
    skip_row = jnp.dot(
        jnp.broadcast_to(skip_ref[...], (8, heads)), jnp.where(twice, 1.0, 0.0).astype(F32),
        precision=lax.Precision.HIGHEST, preferred_element_type=F32,
    )[0:1]

    def split(x):
        high = x.astype(BF16).astype(F32)
        return jnp.where(lane < heads, high, x - high).astype(BF16)

    small = [skip_row]
    halves, totals, befores = [], [], []
    running = jnp.zeros((1, 2 * heads), F32)
    for k in range(blocks):
        span = slice(k * Q, (k + 1) * Q)
        decay = ld_ref[:, span]
        decay = jnp.concatenate([decay, decay], axis=0)
        cum = lax.dot_general(
            ones_lower, decay, (((1,), (1,)), ((), ())),
            precision=lax.Precision.HIGHEST, preferred_element_type=F32,
        )
        total = cum[Q - 1:Q]
        half = 0.5 * total
        lhs_buf[2 * k * Q:(2 * k + 1) * Q, :] = split(jnp.exp(cum - half))
        lhs_buf[(2 * k + 1) * Q:(2 * k + 2) * Q, :] = split(jnp.exp(half - cum))
        running = running + total
        halves.append(jnp.exp(half))
        totals.append(jnp.exp(total))
        befores.append(jnp.exp(running))
        b_block = b_ref[span, :]
        scores = lax.dot_general(
            c_ref[span, :], b_block, (((1,), (1,)), ((), ())), preferred_element_type=F32
        )
        sb_buf[k, 0:Q, :] = jnp.where(lower, scores, 0.0).astype(BF16)
        sb_buf[k, Q:Q + state_dim, :] = b_block.astype(F32).T.astype(BF16)
    small = [skip_row] + halves + totals + befores
    row_count = row_buf.shape[1]
    row_id = lax.broadcasted_iota(jnp.int32, (row_count, 2 * heads), 0)
    stacked = jnp.zeros((row_count, 2 * heads), F32)
    for i, row in enumerate(small):
        stacked = jnp.where(row_id == i, row, stacked)
    base = 2 * blocks * Q
    lhs_buf[base:base + row_count, :] = split(stacked)

    @pl.when(rung == 0)
    def _():
        z_in[...] = jnp.zeros_like(z_in)

    peers = 2 + len(far) + jnp.where(rung > 0, 1, 0) + jnp.where(rung < rungs - 1, 1, 0)
    pl.semaphore_wait(barrier, peers)
    loads[-1].wait()

    def x_copy(g):
        return pltpu.make_async_remote_copy(
            x_out.at[g], x_in.at[g], xs.at[g], xr.at[g], device_id=across, device_id_type=MESH)

    def z_copy(g):
        return pltpu.make_async_remote_copy(
            z_out.at[g], z_in.at[g], zs.at[g], zr.at[g], device_id=above, device_id_type=MESH)

    def far_copy(j, g):
        return pltpu.make_async_remote_copy(
            o_buf.at[g], gathered.at[doc, g], ys.at[j, g], yr.at[j, g],
            device_id=far[j], device_id_type=MESH)

    def twin_copy(g):
        return pltpu.make_async_remote_copy(
            o_buf.at[g], gathered.at[doc, g], cs.at[g], cr.at[g],
            device_id=twin, device_id_type=MESH)

    def own_copy(g):
        return pltpu.make_async_copy(o_buf.at[g], gathered.at[doc, g], own_sem.at[g])

    def forward_copy(j, g):
        source = ((side + sides - 1 - j) % sides) * 2 + core
        return pltpu.make_async_remote_copy(
            gathered.at[source, g], gathered.at[source, g], fs.at[j, g], fr.at[j, g],
            device_id=twin, device_id_type=MESH)

    def local_part(g, carry):
        lanes = pl.ds(pl.multiple_of(g * width, width), width)
        head_of = lax.broadcasted_iota(jnp.int32, (2 * heads, width), 1) // head_dim
        head_at = lax.broadcasted_iota(jnp.int32, (2 * heads, width), 0) % heads
        spread = jnp.where(head_at == head_of + g * (width // head_dim), 1.0, 0.0).astype(BF16)
        rows = jnp.dot(lhs_buf[base:base + row_count, :], spread, preferred_element_type=F32)
        row_buf[g] = rows
        state = jnp.zeros((state_dim, width), F32)
        for k in range(blocks):
            a_buf[g, k * Q:(k + 1) * Q, :] = jnp.dot(
                lhs_buf[2 * k * Q:(2 * k + 1) * Q, :], spread, preferred_element_type=F32)
            grow = jnp.dot(
                lhs_buf[(2 * k + 1) * Q:(2 * k + 2) * Q, :], spread, preferred_element_type=F32)
            scaled = (v_buf[k * Q:(k + 1) * Q, lanes].astype(F32) * grow).astype(BF16)
            both = jnp.dot(sb_buf[k], scaled, preferred_element_type=F32)
            d_buf[g, k * Q:(k + 1) * Q, :] = both[0:Q]
            state = rows[1 + blocks + k:2 + blocks + k] * state + rows[1 + k:2 + k] * both[Q:]
            l_buf[k, g] = state
        x_out[g, 0:state_dim, :] = state.astype(BF16)
        decay = rows[3 * blocks:3 * blocks + 1]
        high = decay.astype(BF16).astype(F32)
        tail = lax.broadcasted_iota(jnp.int32, (16, width), 0)
        x_out[g, state_dim:state_dim + 16, :] = jnp.where(
            tail == 0, high, jnp.where(tail == 1, decay - high, 0.0)).astype(BF16)
        x_copy(g).start()
        return carry

    ahead = min(3, chunks // group)
    lax.fori_loop(0, ahead * group, local_part, 0)

    def carried_part(step, part):
        g = step * group + part
        lanes = pl.ds(pl.multiple_of(g * width, width), width)
        o_lanes = pl.ds(part * width, width)
        rows = row_buf[g]
        x_copy(g).wait_recv()
        other = x_in[g, 0:state_dim, :].astype(F32)
        other_tail = x_in[g, state_dim:state_dim + 16, :].astype(F32)
        other_decay = other_tail[0:1] + other_tail[1:2]
        mine = l_buf[blocks - 1, g]
        mine_decay = rows[3 * blocks:3 * blocks + 1]
        is_second = second == 1
        first_state = jnp.where(is_second, other, mine)
        last_state = jnp.where(is_second, mine, other)
        first_decay = jnp.where(is_second, other_decay, mine_decay)
        last_decay = jnp.where(is_second, mine_decay, other_decay)

        @pl.when(rung > 0)
        def _():
            z_copy(g).wait_recv()

        enter = z_in[g].astype(F32)
        middle = first_decay * enter + first_state

        @pl.when(rung < rungs - 1)
        def _():
            z_out[g] = (last_decay * middle + last_state).astype(BF16)
            z_copy(g).start()

        enter = jnp.where(is_second, middle, enter)
        skip_lanes = rows[0:1]
        for k in range(blocks):
            span = slice(k * Q, (k + 1) * Q)
            at_block = enter
            if k > 0:
                at_block = rows[2 * blocks + k:2 * blocks + k + 1] * enter + l_buf[k - 1, g]
            scaled = (rows[1 + k:2 + k] * at_block).astype(BF16)
            inner = d_buf[g, span, :] + jnp.dot(
                c_ref[span, :], scaled, preferred_element_type=F32)
            o_buf[g // group, span, o_lanes] = (
                a_buf[g, span, :] * inner + skip_lanes * v_buf[span, lanes].astype(F32)
            ).astype(BF16)

    def send(step):
        for j in range(len(far)):
            far_copy(j, step).start()
        twin_copy(step).start()
        own_copy(step).start()

    def outputs(step, carry):
        for part in range(group):
            carried_part(step, part)
        send(step)
        return carry

    def outputs_and_later(step, carry):
        outputs(step, carry)
        for part in range(group):
            local_part((step + ahead) * group + part, carry)
        return carry

    steps = chunks // group
    lax.fori_loop(0, steps - ahead, outputs_and_later, 0)
    lax.fori_loop(steps - ahead, steps, outputs, 0)

    def forward(g, carry):
        for j in range(len(far)):
            far_copy(j, g).wait_recv()
            forward_copy(j, g).start()
        return carry

    lax.fori_loop(0, steps, forward, 0)

    def finish(g, carry):
        for j in range(len(far)):
            far_copy(j, g).wait_send()
            forward_copy(j, g).wait()
        twin_copy(g).wait()
        own_copy(g).wait()
        return carry

    lax.fori_loop(0, steps, finish, 0)

    def finish_states(g, carry):
        x_copy(g).wait_send()

        @pl.when(rung < rungs - 1)
        def _():
            z_copy(g).wait_send()

        return carry

    lax.fori_loop(0, chunks, finish_states, 0)


def pick_kernel(blocks, owner, me, taken, out, zeros, held, flat, load_sem, store_sem):
    chunks, width = taken.shape[1], taken.shape[3]
    slots = out.shape[1]
    places = []
    for i in range(slots):
        doc, rank = i // CAP, i % CAP
        seen = jnp.int32(0)
        block = jnp.int32(0)
        present = jnp.bool_(False)
        for j in range(blocks):
            match = owner[j, doc] == me[0]
            hit = match & (seen == rank)
            block = jnp.where(hit, j, block)
            present = present | hit
            seen = seen + match.astype(jnp.int32)
        places.append(present)
        rows = pl.ds(pl.multiple_of(block * Q, Q), Q)

        @pl.when(present)
        def _():
            pltpu.make_async_copy(
                taken.at[doc, :, rows, :], held.at[i], load_sem.at[i]
            ).start()

    zeros[...] = jnp.zeros_like(zeros)
    for i, present in enumerate(places):

        @pl.when(jnp.logical_not(present))
        def _():
            pltpu.make_async_copy(zeros, out.at[0, i], store_sem.at[i]).start()

    for i, present in enumerate(places):

        @pl.when(present)
        def _():
            pltpu.make_async_copy(held.at[i], held.at[i], load_sem.at[i]).wait()

            def relay(g, carry):
                flat[i, :, pl.ds(pl.multiple_of(g * width, width), width)] = held[i, g]
                return carry

            lax.fori_loop(0, chunks, relay, 0)
            pltpu.make_async_copy(flat.at[i], out.at[0, i], store_sem.at[i]).start()

    for i in range(slots):
        pltpu.make_async_copy(zeros, out.at[0, i], store_sem.at[i]).wait()


def local(n_seq, n_doc, values, b_in, c_in, log_decay, skip, owner):
    seq_len, row_width = values.shape[1], values.shape[2]
    heads = log_decay.shape[1]
    state_dim = b_in.shape[2]
    blocks = seq_len // Q
    group = 1
    width = 128
    chunks = row_width // width
    steps, step_width = chunks // group, width * group
    far = n_doc // 2 - 1
    row_count = -(-(1 + 3 * blocks) // 16) * 16
    smem = pl.BlockSpec(memory_space=pltpu.SMEM)
    anywhere = pl.BlockSpec(memory_space=pl.ANY)
    dma = pltpu.SemaphoreType.DMA
    gathered = pl.pallas_call(
        functools.partial(layer_kernel, n_seq, n_doc, heads, width, chunks, group),
        out_shape=jax.ShapeDtypeStruct((n_doc, steps, seq_len, step_width), BF16),
        in_specs=[anywhere] * 5,
        out_specs=anywhere,
        scratch_shapes=[
            pltpu.VMEM((seq_len, row_width), BF16),
            pltpu.VMEM((seq_len, state_dim), BF16),
            pltpu.VMEM((seq_len, state_dim), BF16),
            pltpu.VMEM((heads, seq_len), F32),
            pltpu.VMEM((1, heads), F32),
            pltpu.VMEM((2 * seq_len + row_count, 2 * heads), BF16),
            pltpu.VMEM((blocks, Q + state_dim, Q), BF16),
            pltpu.VMEM((chunks, seq_len, width), F32),
            pltpu.VMEM((chunks, seq_len, width), F32),
            pltpu.VMEM((chunks, row_count, width), F32),
            pltpu.VMEM((blocks, chunks, state_dim, width), F32),
            pltpu.VMEM((chunks, state_dim + 16, width), BF16),
            pltpu.VMEM((chunks, state_dim + 16, width), BF16),
            pltpu.VMEM((chunks, state_dim, width), BF16),
            pltpu.VMEM((chunks, state_dim, width), BF16),
            pltpu.VMEM((steps, seq_len, step_width), BF16),
            dma((5,)),
            dma((steps,)),
            dma((chunks,)),
            dma((chunks,)),
            dma((chunks,)),
            dma((chunks,)),
            dma((far, steps)),
            dma((far, steps)),
            dma((steps,)),
            dma((steps,)),
            dma((far, steps)),
            dma((far, steps)),
        ],
        compiler_params=pltpu.CompilerParams(
            collective_id=0, has_side_effects=True, vmem_limit_bytes=60 * 2**20
        ),
        name="layer",
    )(values[0], b_in[0], c_in[0], log_decay[0], skip.reshape(1, heads))

    slots = n_doc * CAP
    me = lax.axis_index("doc").astype(jnp.int32).reshape(1)

    return pl.pallas_call(
        functools.partial(pick_kernel, blocks),
        out_shape=jax.ShapeDtypeStruct((1, slots, Q, row_width), BF16),
        in_specs=[smem, smem, anywhere],
        out_specs=anywhere,
        scratch_shapes=[
            pltpu.VMEM((Q, row_width), BF16),
            pltpu.VMEM((slots, steps, Q, step_width), BF16),
            pltpu.VMEM((slots, Q, row_width), BF16),
            dma((slots,)),
            dma((slots,)),
        ],
        compiler_params=pltpu.CompilerParams(vmem_limit_bytes=60 * 2**20),
        name="pick",
    )(owner.T, me, gathered)


def solution(mesh):
    in_specs = (
        P("doc", "seq", None),
        P("doc", "seq", None),
        P("doc", "seq", None),
        P("doc", None, "seq"),
        P(),
        P(None, "seq"),
    )
    out_specs = P("doc", "seq", None, None)
    body = functools.partial(local, mesh.shape["seq"], mesh.shape["doc"])
    return jax.shard_map(body, mesh=mesh, in_specs=in_specs, out_specs=out_specs, check_vma=False)
```

```python
import functools

import jax
import jax.numpy as jnp
from jax import lax
from jax.experimental import pallas as pl
from jax.experimental.pallas import tpu as pltpu
from jax.sharding import PartitionSpec as P

Q = 128
CAP = 2
MESH = pl.DeviceIdType.MESH
F32 = jnp.float32
BF16 = jnp.bfloat16


def layer_kernel(
    n_seq, n_doc, heads, width, chunks, group,
    v_hbm, b_hbm, c_hbm, ld_hbm, skip_hbm, gathered,
    v_buf, b_ref, c_ref, ld_ref, skip_ref, lhs_buf, sb_buf, a_buf, d_buf, row_buf, l_buf, x_out, x_in, p_out, p_in, e_out, e_in, o_buf,
    in_sem, own_sem, xs, xr, ps, pr, es, e2s, er, ys, yr, cs, cr, fs, fr,
):
    seq_len, row_width = v_buf.shape
    blocks = seq_len // Q
    state_dim = b_ref.shape[1]
    head_dim = row_width // heads
    sides = n_doc // 2
    rungs = n_seq // 2
    seq = lax.axis_index("seq")
    doc = lax.axis_index("doc")
    rung, second = seq // 2, seq % 2
    side, core = doc // 2, doc % 2
    across = (seq + 1 - 2 * second, doc)
    above = (seq + 2, doc)
    below = (seq - 2, doc)
    above2 = (seq + 4, doc)
    below2 = (seq - 4, doc)
    odd = rung % 2 == 1
    head_start = p_in.shape[0]
    has_above = rung < rungs - 1
    sends_p = jnp.logical_not(odd) & has_above
    sends_e = odd & has_above
    sends_e2 = odd & (rung < rungs - 2)
    takes_e = rung > 1
    from_below2 = odd & takes_e
    twin = (seq, doc + 1 - 2 * core)
    far = [(seq, ((side + j) % sides) * 2 + core) for j in range(1, sides)]

    pairs = [(ld_hbm, ld_ref), (skip_hbm, skip_ref), (b_hbm, b_ref), (c_hbm, c_ref), (v_hbm, v_buf)]
    loads = [pltpu.make_async_copy(a, b, in_sem.at[i]) for i, (a, b) in enumerate(pairs)]
    for load in loads:
        load.start()

    barrier = pltpu.get_barrier_semaphore()
    for other in [across, twin] + far:
        pl.semaphore_signal(barrier, inc=1, device_id=other, device_id_type=MESH)

    @pl.when(rung > 0)
    def _():
        pl.semaphore_signal(barrier, inc=1, device_id=below, device_id_type=MESH)

    @pl.when(has_above)
    def _():
        pl.semaphore_signal(barrier, inc=1, device_id=above, device_id_type=MESH)

    @pl.when(sends_e2)
    def _():
        pl.semaphore_signal(barrier, inc=1, device_id=above2, device_id_type=MESH)

    @pl.when(from_below2)
    def _():
        pl.semaphore_signal(barrier, inc=1, device_id=below2, device_id_type=MESH)

    for load in loads[:-1]:
        load.wait()

    rows_i = lax.broadcasted_iota(jnp.int32, (Q, Q), 0)
    cols_i = lax.broadcasted_iota(jnp.int32, (Q, Q), 1)
    lower = rows_i >= cols_i
    ones_lower = jnp.where(lower, 1.0, 0.0).astype(F32)
    lane = lax.broadcasted_iota(jnp.int32, (1, 2 * heads), 1)
    twice = (
        lax.broadcasted_iota(jnp.int32, (heads, 2 * heads), 1) % heads
        == lax.broadcasted_iota(jnp.int32, (heads, 2 * heads), 0)
    )
    skip_row = jnp.dot(
        jnp.broadcast_to(skip_ref[...], (8, heads)), jnp.where(twice, 1.0, 0.0).astype(F32),
        precision=lax.Precision.HIGHEST, preferred_element_type=F32,
    )[0:1]

    def split(x):
        high = x.astype(BF16).astype(F32)
        return jnp.where(lane < heads, high, x - high).astype(BF16)

    small = [skip_row]
    halves, totals, befores = [], [], []
    running = jnp.zeros((1, 2 * heads), F32)
    for k in range(blocks):
        span = slice(k * Q, (k + 1) * Q)
        decay = ld_ref[:, span]
        decay = jnp.concatenate([decay, decay], axis=0)
        cum = lax.dot_general(
            ones_lower, decay, (((1,), (1,)), ((), ())),
            precision=lax.Precision.HIGHEST, preferred_element_type=F32,
        )
        total = cum[Q - 1:Q]
        half = 0.5 * total
        lhs_buf[2 * k * Q:(2 * k + 1) * Q, :] = split(jnp.exp(cum - half))
        lhs_buf[(2 * k + 1) * Q:(2 * k + 2) * Q, :] = split(jnp.exp(half - cum))
        running = running + total
        halves.append(jnp.exp(half))
        totals.append(jnp.exp(total))
        befores.append(jnp.exp(running))
        b_block = b_ref[span, :]
        scores = lax.dot_general(
            c_ref[span, :], b_block, (((1,), (1,)), ((), ())), preferred_element_type=F32
        )
        sb_buf[k, 0:Q, :] = jnp.where(lower, scores, 0.0).astype(BF16)
        sb_buf[k, Q:Q + state_dim, :] = b_block.astype(F32).T.astype(BF16)
    small = [skip_row] + halves + totals + befores
    row_count = row_buf.shape[1]
    row_id = lax.broadcasted_iota(jnp.int32, (row_count, 2 * heads), 0)
    stacked = jnp.zeros((row_count, 2 * heads), F32)
    for i, row in enumerate(small):
        stacked = jnp.where(row_id == i, row, stacked)
    base = 2 * blocks * Q
    lhs_buf[base:base + row_count, :] = split(stacked)

    @pl.when(rung == 0)
    def _():
        e_in[...] = jnp.zeros_like(e_in)

    @pl.when(rung == 1)
    def _():
        e_in[0:head_start] = jnp.zeros((head_start, state_dim, width), BF16)

    @pl.when(jnp.logical_not(odd))
    def _():
        p_in[...] = jnp.zeros_like(p_in)

    peers = 2 + len(far) + jnp.where(rung > 0, 1, 0) + jnp.where(has_above, 1, 0)
    peers = peers + jnp.where(sends_e2, 1, 0) + jnp.where(from_below2, 1, 0)
    pl.semaphore_wait(barrier, peers)
    loads[-1].wait()

    def x_copy(g):
        return pltpu.make_async_remote_copy(
            x_out.at[g], x_in.at[g], xs.at[g], xr.at[g], device_id=across, device_id_type=MESH)

    def p_copy(g):
        return pltpu.make_async_remote_copy(
            p_out.at[g], p_in.at[g], ps.at[g], pr.at[g], device_id=above, device_id_type=MESH)

    def e_copy(g):
        return pltpu.make_async_remote_copy(
            e_out.at[g], e_in.at[g], es.at[g], er.at[g], device_id=above, device_id_type=MESH)

    def e2_copy(g):
        return pltpu.make_async_remote_copy(
            e_out.at[g], e_in.at[g], e2s.at[g], er.at[g], device_id=above2, device_id_type=MESH)

    def with_decay(buf, g, state, decay):
        high = decay.astype(BF16).astype(F32)
        tail = lax.broadcasted_iota(jnp.int32, (16, width), 0)
        buf[g, 0:state_dim, :] = state.astype(BF16)
        buf[g, state_dim:state_dim + 16, :] = jnp.where(
            tail == 0, high, jnp.where(tail == 1, decay - high, 0.0)).astype(BF16)

    def without_decay(buf, g):
        tail = buf[g, state_dim:state_dim + 16, :].astype(F32)
        return buf[g, 0:state_dim, :].astype(F32), tail[0:1] + tail[1:2]

    def far_copy(j, g):
        return pltpu.make_async_remote_copy(
            o_buf.at[g], gathered.at[doc, g], ys.at[j, g], yr.at[j, g],
            device_id=far[j], device_id_type=MESH)

    def twin_copy(g):
        return pltpu.make_async_remote_copy(
            o_buf.at[g], gathered.at[doc, g], cs.at[g], cr.at[g],
            device_id=twin, device_id_type=MESH)

    def own_copy(g):
        return pltpu.make_async_copy(o_buf.at[g], gathered.at[doc, g], own_sem.at[g])

    def forward_copy(j, g):
        source = ((side + sides - 1 - j) % sides) * 2 + core
        return pltpu.make_async_remote_copy(
            gathered.at[source, g], gathered.at[source, g], fs.at[j, g], fr.at[j, g],
            device_id=twin, device_id_type=MESH)

    def local_part(g, carry):
        lanes = pl.ds(pl.multiple_of(g * width, width), width)
        head_of = lax.broadcasted_iota(jnp.int32, (2 * heads, width), 1) // head_dim
        head_at = lax.broadcasted_iota(jnp.int32, (2 * heads, width), 0) % heads
        spread = jnp.where(head_at == head_of + g * (width // head_dim), 1.0, 0.0).astype(BF16)
        rows = jnp.dot(lhs_buf[base:base + row_count, :], spread, preferred_element_type=F32)
        row_buf[g] = rows
        state = jnp.zeros((state_dim, width), F32)
        for k in range(blocks):
            a_buf[g, k * Q:(k + 1) * Q, :] = jnp.dot(
                lhs_buf[2 * k * Q:(2 * k + 1) * Q, :], spread, preferred_element_type=F32)
            grow = jnp.dot(
                lhs_buf[(2 * k + 1) * Q:(2 * k + 2) * Q, :], spread, preferred_element_type=F32)
            scaled = (v_buf[k * Q:(k + 1) * Q, lanes].astype(F32) * grow).astype(BF16)
            both = jnp.dot(sb_buf[k], scaled, preferred_element_type=F32)
            d_buf[g, k * Q:(k + 1) * Q, :] = both[0:Q]
            state = rows[1 + blocks + k:2 + blocks + k] * state + rows[1 + k:2 + k] * both[Q:]
            l_buf[k, g] = state
        with_decay(x_out, g, state, rows[3 * blocks:3 * blocks + 1])
        x_copy(g).start()
        return carry

    ahead = min(2, chunks // group)
    lax.fori_loop(0, ahead * group, local_part, 0)

    def carried_part(step, part, early):
        g = step * group + part
        lanes = pl.ds(pl.multiple_of(g * width, width), width)
        o_lanes = pl.ds(part * width, width)
        rows = row_buf[g]
        x_copy(g).wait_recv()
        other, other_decay = without_decay(x_in, g)
        mine = l_buf[blocks - 1, g]
        mine_decay = rows[3 * blocks:3 * blocks + 1]
        is_second = second == 1
        first_state = jnp.where(is_second, other, mine)
        last_state = jnp.where(is_second, mine, other)
        first_decay = jnp.where(is_second, other_decay, mine_decay)
        last_decay = jnp.where(is_second, mine_decay, other_decay)

        if early:

            @pl.when(sends_p)
            def _():
                pair_state = last_decay * first_state + last_state
                with_decay(p_out, g, pair_state, first_decay * last_decay)
                p_copy(g).start()

        if early:

            @pl.when(odd)
            def _():
                p_copy(g).wait_recv()

        @pl.when(takes_e if early else rung > 0)
        def _():
            e_copy(g).wait_recv()

        enter = e_in[g].astype(F32)
        if early:
            under, under_decay = without_decay(p_in, g)
            enter = jnp.where(odd, under_decay * enter + under, enter)
        middle = first_decay * enter + first_state
        sends = sends_e if early else has_above

        @pl.when(sends)
        def _():
            e_out[g] = (last_decay * middle + last_state).astype(BF16)

        if early:

            @pl.when(sends_e2)
            def _():
                e2_copy(g).start()

        @pl.when(sends)
        def _():
            e_copy(g).start()

        enter = jnp.where(is_second, middle, enter)
        skip_lanes = rows[0:1]
        for k in range(blocks):
            span = slice(k * Q, (k + 1) * Q)
            at_block = enter
            if k > 0:
                at_block = rows[2 * blocks + k:2 * blocks + k + 1] * enter + l_buf[k - 1, g]
            scaled = (rows[1 + k:2 + k] * at_block).astype(BF16)
            inner = d_buf[g, span, :] + jnp.dot(
                c_ref[span, :], scaled, preferred_element_type=F32)
            o_buf[g // group, span, o_lanes] = (
                a_buf[g, span, :] * inner + skip_lanes * v_buf[span, lanes].astype(F32)
            ).astype(BF16)

    def send(step):
        for j in range(len(far)):
            far_copy(j, step).start()
        twin_copy(step).start()
        own_copy(step).start()

    def outputs(early, step, carry):
        for part in range(group):
            carried_part(step, part, early)
        send(step)
        return carry

    def outputs_and_later(early, step, carry):
        outputs(early, step, carry)
        for part in range(group):
            local_part((step + ahead) * group + part, carry)
        return carry

    steps = chunks // group
    first = head_start // group
    lax.fori_loop(0, first, functools.partial(outputs_and_later, True), 0)
    lax.fori_loop(first, steps - ahead, functools.partial(outputs_and_later, False), 0)
    lax.fori_loop(steps - ahead, steps, functools.partial(outputs, False), 0)

    def forward(g, carry):
        for j in range(len(far)):
            far_copy(j, g).wait_recv()
            forward_copy(j, g).start()
        return carry

    lax.fori_loop(0, steps, forward, 0)

    def finish(g, carry):
        for j in range(len(far)):
            far_copy(j, g).wait_send()
            forward_copy(j, g).wait()
        twin_copy(g).wait()
        own_copy(g).wait()
        return carry

    lax.fori_loop(0, steps, finish, 0)

    def finish_states(g, carry):
        x_copy(g).wait_send()
        return carry

    lax.fori_loop(0, chunks, finish_states, 0)

    def finish_first(g, carry):
        @pl.when(sends_p)
        def _():
            p_copy(g).wait_send()

        @pl.when(sends_e)
        def _():
            e_copy(g).wait_send()

        @pl.when(sends_e2)
        def _():
            e2_copy(g).wait_send()

        return carry

    lax.fori_loop(0, head_start, finish_first, 0)

    def finish_chain(g, carry):
        @pl.when(has_above)
        def _():
            e_copy(g).wait_send()

        return carry

    lax.fori_loop(head_start, chunks, finish_chain, 0)


def pick_kernel(blocks, owner, me, taken, out, zeros, held, flat, load_sem, store_sem):
    chunks, width = taken.shape[1], taken.shape[3]
    slots = out.shape[1]
    places = []
    for i in range(slots):
        doc, rank = i // CAP, i % CAP
        seen = jnp.int32(0)
        block = jnp.int32(0)
        present = jnp.bool_(False)
        for j in range(blocks):
            match = owner[j, doc] == me[0]
            hit = match & (seen == rank)
            block = jnp.where(hit, j, block)
            present = present | hit
            seen = seen + match.astype(jnp.int32)
        places.append(present)
        rows = pl.ds(pl.multiple_of(block * Q, Q), Q)

        @pl.when(present)
        def _():
            pltpu.make_async_copy(
                taken.at[doc, :, rows, :], held.at[i], load_sem.at[i]
            ).start()

    zeros[...] = jnp.zeros_like(zeros)
    for i, present in enumerate(places):

        @pl.when(jnp.logical_not(present))
        def _():
            pltpu.make_async_copy(zeros, out.at[0, i], store_sem.at[i]).start()

    for i, present in enumerate(places):

        @pl.when(present)
        def _():
            pltpu.make_async_copy(held.at[i], held.at[i], load_sem.at[i]).wait()

            def relay(g, carry):
                flat[i, :, pl.ds(pl.multiple_of(g * width, width), width)] = held[i, g]
                return carry

            lax.fori_loop(0, chunks, relay, 0)
            pltpu.make_async_copy(flat.at[i], out.at[0, i], store_sem.at[i]).start()

    for i in range(slots):
        pltpu.make_async_copy(zeros, out.at[0, i], store_sem.at[i]).wait()


def local(n_seq, n_doc, values, b_in, c_in, log_decay, skip, owner):
    seq_len, row_width = values.shape[1], values.shape[2]
    heads = log_decay.shape[1]
    state_dim = b_in.shape[2]
    blocks = seq_len // Q
    group = 2
    width = 128
    chunks = row_width // width
    steps, step_width = chunks // group, width * group
    head_start = min(2, steps - 2) * group
    far = n_doc // 2 - 1
    row_count = -(-(1 + 3 * blocks) // 16) * 16
    smem = pl.BlockSpec(memory_space=pltpu.SMEM)
    anywhere = pl.BlockSpec(memory_space=pl.ANY)
    dma = pltpu.SemaphoreType.DMA
    gathered = pl.pallas_call(
        functools.partial(layer_kernel, n_seq, n_doc, heads, width, chunks, group),
        out_shape=jax.ShapeDtypeStruct((n_doc, steps, seq_len, step_width), BF16),
        in_specs=[anywhere] * 5,
        out_specs=anywhere,
        scratch_shapes=[
            pltpu.VMEM((seq_len, row_width), BF16),
            pltpu.VMEM((seq_len, state_dim), BF16),
            pltpu.VMEM((seq_len, state_dim), BF16),
            pltpu.VMEM((heads, seq_len), F32),
            pltpu.VMEM((1, heads), F32),
            pltpu.VMEM((2 * seq_len + row_count, 2 * heads), BF16),
            pltpu.VMEM((blocks, Q + state_dim, Q), BF16),
            pltpu.VMEM((chunks, seq_len, width), F32),
            pltpu.VMEM((chunks, seq_len, width), F32),
            pltpu.VMEM((chunks, row_count, width), F32),
            pltpu.VMEM((blocks, chunks, state_dim, width), F32),
            pltpu.VMEM((chunks, state_dim + 16, width), BF16),
            pltpu.VMEM((chunks, state_dim + 16, width), BF16),
            pltpu.VMEM((head_start, state_dim + 16, width), BF16),
            pltpu.VMEM((head_start, state_dim + 16, width), BF16),
            pltpu.VMEM((chunks, state_dim, width), BF16),
            pltpu.VMEM((chunks, state_dim, width), BF16),
            pltpu.VMEM((steps, seq_len, step_width), BF16),
            dma((5,)),
            dma((steps,)),
            dma((chunks,)),
            dma((chunks,)),
            dma((chunks,)),
            dma((chunks,)),
            dma((chunks,)),
            dma((chunks,)),
            dma((chunks,)),
            dma((far, steps)),
            dma((far, steps)),
            dma((steps,)),
            dma((steps,)),
            dma((far, steps)),
            dma((far, steps)),
        ],
        compiler_params=pltpu.CompilerParams(
            collective_id=0, has_side_effects=True, vmem_limit_bytes=60 * 2**20
        ),
        name="layer",
    )(values[0], b_in[0], c_in[0], log_decay[0], skip.reshape(1, heads))

    slots = n_doc * CAP
    me = lax.axis_index("doc").astype(jnp.int32).reshape(1)

    return pl.pallas_call(
        functools.partial(pick_kernel, blocks),
        out_shape=jax.ShapeDtypeStruct((1, slots, Q, row_width), BF16),
        in_specs=[smem, smem, anywhere],
        out_specs=anywhere,
        scratch_shapes=[
            pltpu.VMEM((Q, row_width), BF16),
            pltpu.VMEM((slots, steps, Q, step_width), BF16),
            pltpu.VMEM((slots, Q, row_width), BF16),
            dma((slots,)),
            dma((slots,)),
        ],
        compiler_params=pltpu.CompilerParams(vmem_limit_bytes=60 * 2**20),
        name="pick",
    )(owner.T, me, gathered)


def solution(mesh):
    in_specs = (
        P("doc", "seq", None),
        P("doc", "seq", None),
        P("doc", "seq", None),
        P("doc", None, "seq"),
        P(),
        P(None, "seq"),
    )
    out_specs = P("doc", "seq", None, None)
    body = functools.partial(local, mesh.shape["seq"], mesh.shape["doc"])
    return jax.shard_map(body, mesh=mesh, in_specs=in_specs, out_specs=out_specs, check_vma=False)
```
